32 devices in a mesh: tm: 2 (over x), rows: 16 (over z, y, core).
Axes of the slice: x: 2, y: 2, z: 4, core: 2. Of those that a mesh axis runs over, the one named last changes fastest.
Arguments:
- inverse_block: bfloat16 [2, 2048, 2048], P('tm', 'rows'), may hold values from -6 to 6
- coupling_tiles: bfloat16 [2, 64, 128, 128], P('tm', 'rows'), may hold values from -0.005859375 to 0.005859375
- tile_pos: int32 [2, 64, 2], P('tm', 'rows'), may hold values from 0 to 31, as said below
- sep_diag: bfloat16 [2, 2048, 2048], P('tm', 'rows'), as said below
- sep_cross: bfloat16 [2, 2048, 2048], P('tm', 'rows')
Outputs:
- sigma_es: float32 [2, 2048, 4096], P('tm', 'rows')
- sigma_tiles: float32 [2, 2048, 128], P('tm', 'rows')
The draws below stay inside these ranges and needn't reach their ends.
Inputs may be any that keep to these rules, and one draw needn't show every extreme that they name: `tile_pos`: within one block the K pairs (tile row, tile column) are distinct; tile rows are below 16, tile columns below 32. `sep_diag`: each block is symmetric.
All inputs are finite; a program needn't handle non-finite values.
Results may differ from the reference program's by a relative error of at most 0.0034.
Values may be sent and summed in bfloat16 or wider, within the bound.
No kernel may reach another device: no remote copies, remote signals or barrier semaphores. Data moves between devices by JAX's collectives and lax.ppermute only.
A program may use at most 128 MiB of HBM per device.

```python
import jax
import jax.numpy as jnp
from jax import lax

N = 2048
TILE = 128
G = 2
K = 64


def draw_tile_pos(key, part):
    key = jax.random.fold_in(key, 11)
    cols = 2 * N // TILE
    cells = N // TILE * cols

    def one(sub):
        inner = jax.random.permutation(sub, cells - 2)[:K - 2] + 1
        chosen = jnp.concatenate([jnp.array([0, cells - 1], jnp.int32), inner.astype(jnp.int32)])
        chosen = jax.random.permutation(jax.random.fold_in(sub, 5), chosen)
        return jnp.stack([chosen // cols, chosen % cols], axis=1).astype(jnp.int32)
    keys = jax.random.split(key, G)
    return jax.vmap(one)(keys)


def symmetric_block(key):
    base = jax.random.normal(key, (G, N, N), jnp.float32)
    return (base + jnp.swapaxes(base, 1, 2)) * 0.7071


def draw_sep_diag(key, part):
    key = jax.random.fold_in(key, 23)
    return symmetric_block(key).astype(jnp.bfloat16)


def draw_sep_cross(key, part):
    key = jax.random.fold_in(key, 37)
    base = jax.random.normal(key, (G, N, N), jnp.float32)
    return base.astype(jnp.bfloat16)


def level_of(key, dims, pieces, low, top_value):
    def one(axis_at, shards_of):
        draws = jax.random.uniform(jax.random.fold_in(jax.random.fold_in(key, 6), axis_at), (shards_of,), jnp.float32, low / len(pieces), top_value / len(pieces))
        return jnp.repeat(jnp.exp(draws), dims[axis_at] // shards_of).reshape((-1,) + (1,) * (len(dims) - axis_at - 1))

    gain = one(*pieces[0])
    for cut in pieces[1:]:
        gain = gain * one(*cut)
    return gain


def normal_values(key, shape, width, most, shards=(), dtype=jnp.bfloat16):
    gain = level_of(key, shape, shards, -0.22, 0.18) if shards else 1.0
    entries = jax.random.normal(key, shape, jnp.float32) * width * gain
    return jnp.minimum(jnp.maximum(entries, -most), most).astype(dtype)


def setup_inputs(seed: int = 0) -> dict:
    key_list = jax.random.split(jax.random.key(seed), 6)
    return {
        "inverse_block": normal_values(key_list[0], (G, N, N), 1.0, 6.0, ((0, 2), (1, 16))),
        "coupling_tiles": normal_values(key_list[1], (G, K, TILE, TILE), (K * TILE * TILE) ** -0.5, 0.005859375, ((0, 2), (1, 16))),
        "tile_pos": draw_tile_pos(jax.random.fold_in(key_list[5], 71), 0),
        "sep_diag": draw_sep_diag(jax.random.fold_in(key_list[5], 71), 0),
        "sep_cross": draw_sep_cross(jax.random.fold_in(key_list[5], 71), 0),
    }


def build_coupling(tiles, positions):
    full = jnp.zeros((N, 2 * N), jnp.float32)

    def place(k, acc):
        row_tile = positions[k, 0].astype(jnp.int32)
        col_tile = positions[k, 1].astype(jnp.int32)
        return lax.dynamic_update_slice(acc, tiles[k].astype(jnp.float32), (row_tile * TILE, col_tile * TILE))

    return lax.fori_loop(0, K, place, full)


def reference(inverse_block, coupling_tiles, tile_pos, sep_diag, sep_cross):
    hp = lax.Precision.HIGHEST
    es_list = []
    tile_list = []
    count = N // TILE
    for group in range(G):
        winv = inverse_block[group].astype(jnp.float32)
        coupling = build_coupling(coupling_tiles[group], tile_pos[group])
        factor = jnp.dot(winv, coupling, precision=hp).astype(jnp.bfloat16).astype(jnp.float32)
        left = sep_diag[group].astype(jnp.float32)
        cross = sep_cross[group].astype(jnp.float32)
        if group + 1 < G:
            right = sep_diag[group + 1].astype(jnp.float32)
        else:
            right = jnp.zeros((N, N), jnp.float32)
        upper = jnp.concatenate([left, cross], axis=1)
        lower = jnp.concatenate([cross.T, right], axis=1)
        whole = jnp.concatenate([upper, lower], axis=0)
        sigma = -jnp.dot(factor, whole, precision=hp)
        es_list.append(sigma)
        rounded = sigma.astype(jnp.bfloat16).astype(jnp.float32)
        sig_tiles = rounded.reshape(count, TILE, 2 * N)
        fac_tiles = factor.reshape(count, TILE, 2 * N)
        product = jnp.einsum("mrk,mck->mrc", sig_tiles, fac_tiles, precision=hp)
        blocks = winv.reshape(count, TILE, count, TILE)
        diag = jnp.stack([blocks[i, :, i, :] for i in range(count)])
        tile_list.append((diag - product).reshape(N, TILE))
    return jnp.stack(es_list), jnp.stack(tile_list)
```

```python
import functools

import jax
import jax.numpy as jnp
from jax import lax
from jax.experimental import pallas as pl
from jax.experimental.pallas import tpu as pltpu
from jax.sharding import PartitionSpec as P

TILE = 128
PAD = 32
SIDES = 2
CORES = 2
QUAD = SIDES * CORES


def contract_last(left, right):
    return lax.dot_general(
        left, right, (((1,), (1,)), ((), ())), preferred_element_type=jnp.float32
    )


def place(z, y, c):
    return (z * SIDES + y) * CORES + c


def sent(array, line, move):
    pairs = []
    for z in range(line):
        for y in range(SIDES):
            for c in range(CORES):
                target = move(z, y, c)
                if target is not None:
                    pairs.append((place(z, y, c), place(*target)))
    return lax.ppermute(array, "rows", pairs)


def to_core(array, line):
    return sent(array, line, lambda z, y, c: (z, y, 1 - c))


def to_side(array, line):
    return sent(array, line, lambda z, y, c: (z, 1 - y, c))


def hop(array, line, by, low, high):
    def move(z, y, c):
        if low <= z <= high and 0 <= z + by < line:
            return (z + by, y, c)
        return None

    return sent(array, line, move)


def ring_gather(array, line):
    cycle = [(z, 0) for z in range(line)] + [(z, 1) for z in reversed(range(line))]
    where_at = {chip: i for i, chip in enumerate(cycle)}
    count = len(cycle)

    def turn(part, by):
        return sent(
            part, line, lambda z, y, c: (*cycle[(where_at[(z, y)] + by) % count], c)
        )

    pieces = [array]
    ahead = behind = array
    for _ in range(count // 2 - 1):
        ahead = turn(ahead, 1)
        behind = turn(behind, -1)
        pieces += [ahead, behind]
    half = array.shape[0] // 2
    pieces.append(jnp.concatenate([turn(ahead[:half], 1), turn(behind[half:], -1)], axis=0))
    return pieces


def factors_kernel(
    per_shard,
    shards_each,
    pos_ref,
    side_ref,
    near_ref,
    far_ref,
    wrows_ref,
    diag_ref,
    diag_other_ref,
    cross_ref,
    cross_other_ref,
    cols_ref,
    cols_other_ref,
    next_ref,
    next_other_ref,
    updated_ref,
    factor_ref,
    sep_ref,
    wtile_ref,
    sum_ref,
    fac_ref,
):
    rows = wrows_ref.shape[0]
    count = wrows_ref.shape[1] // TILE
    side = side_ref[0]
    mine = pl.ds(pl.multiple_of(side * rows, rows), rows)
    other = pl.ds(pl.multiple_of((1 - side) * rows, rows), rows)
    mine_low = pl.ds(pl.multiple_of((2 + side) * rows, rows), rows)
    other_low = pl.ds(pl.multiple_of((3 - side) * rows, rows), rows)
    for j in range(count):
        lanes = pl.ds(j * TILE, TILE)
        sep_ref[j, mine, :] = diag_ref[:, lanes]
        sep_ref[j, other, :] = diag_other_ref[:, lanes]
        sep_ref[j, mine_low, :] = cols_ref[:, lanes]
        sep_ref[j, other_low, :] = cols_other_ref[:, lanes]
        sep_ref[count + j, mine, :] = cross_ref[:, lanes]
        sep_ref[count + j, other, :] = cross_other_ref[:, lanes]
        sep_ref[count + j, mine_low, :] = next_ref[:, lanes]
        sep_ref[count + j, other_low, :] = next_other_ref[:, lanes]
        wtile_ref[j] = wrows_ref[:, lanes]
    sum_ref[...] = jnp.zeros_like(sum_ref)
    fac_ref[...] = jnp.zeros_like(fac_ref)

    def add(tile, k):
        i = pos_ref[2 * k]
        j = pos_ref[2 * k + 1]
        sum_ref[i] += contract_last(sep_ref[j], tile)
        fac_ref[j] += jnp.dot(wtile_ref[i], tile, preferred_element_type=jnp.float32)

    stride = per_shard * TILE + PAD

    @pl.loop(0, shards_each)
    def _(s):
        for half, ref in enumerate((near_ref, far_ref)):
            for t in range(per_shard):
                start = pl.multiple_of(s * stride + t * TILE, 16)
                add(ref[pl.ds(start, TILE), :], (half * shards_each + s) * per_shard + t)

    for i in range(count):
        updated_ref[:, i * TILE : (i + 1) * TILE] = sum_ref[i].astype(jnp.bfloat16)
    for j in range(2 * count):
        factor_ref[:, j * TILE : (j + 1) * TILE] = fac_ref[j].astype(jnp.bfloat16)


def factors(positions, side, near, far, wrows, seps, per_shard):
    rows, width = wrows.shape
    count = width // TILE
    shards_each = near.shape[0] // (per_shard * TILE + PAD)
    tiles = 2 * shards_each * per_shard
    whole = pl.BlockSpec(memory_space=pltpu.VMEM)
    scalar = pl.BlockSpec(memory_space=pltpu.SMEM)
    return pl.pallas_call(
        functools.partial(factors_kernel, per_shard, shards_each),
        out_shape=(
            jax.ShapeDtypeStruct((4 * rows, width), jnp.bfloat16),
            jax.ShapeDtypeStruct((rows, 2 * width), jnp.bfloat16),
        ),
        in_specs=[scalar, scalar] + [whole] * (3 + len(seps)),
        out_specs=(whole, whole),
        scratch_shapes=[
            pltpu.VMEM((2 * count, 4 * rows, TILE), jnp.bfloat16),
            pltpu.VMEM((count, rows, TILE), jnp.bfloat16),
            pltpu.VMEM((count, 4 * rows, TILE), jnp.float32),
            pltpu.VMEM((2 * count, rows, TILE), jnp.float32),
        ],
        compiler_params=pltpu.CompilerParams(vmem_limit_bytes=48 * 1024 * 1024),
        cost_estimate=pl.CostEstimate(
            flops=2 * tiles * TILE * TILE * rows * 5,
            bytes_accessed=2 * (13 * rows * width + tiles * TILE * TILE),
            transcendentals=0,
        ),
    )(positions, side, near, far, wrows, *seps)


def shards(line, inverse_block, coupling_tiles, tile_pos, sep_diag, sep_cross):
    wrows = inverse_block[0]
    rows, width = wrows.shape
    tiles = coupling_tiles[0]
    per_shard = tiles.shape[0]
    diag = sep_diag[0]
    cross = sep_cross[0]
    index = lax.axis_index("rows")
    z = index // QUAD
    y = index // CORES % SIDES
    c = index % CORES

    marks = tile_pos[0].astype(jnp.bfloat16).reshape(1, -1)
    marks = jnp.pad(marks, ((0, PAD - 1), (0, TILE - marks.shape[1])))
    packed = jnp.concatenate([tiles.reshape(-1, TILE), marks], axis=0)
    near = jnp.concatenate(ring_gather(packed, line), axis=0)
    far = to_core(near, line)

    cols = lax.all_to_all(cross.T, "rows", 0, 1, tiled=True)
    cols_other = to_side(cols, line)

    diag_other = to_side(diag, line)
    cross_other = to_side(cross, line)
    size = lax.axis_size("tm")
    back = [(i + 1, i) for i in range(size - 1)]
    following = lax.ppermute(diag, "tm", back)
    following_other = lax.ppermute(diag_other, "tm", back)

    def marked(part):
        rows_each = per_shard * TILE + PAD
        return part.reshape(-1, rows_each, TILE)[:, per_shard * TILE, : 2 * per_shard]

    positions = jnp.concatenate([marked(near), marked(far)], axis=0)
    positions = positions.astype(jnp.int32).reshape(-1)
    seps = (diag, diag_other, cross, cross_other, cols, cols_other, following, following_other)
    updated, factor = factors(
        positions, y.astype(jnp.int32).reshape(1), near, far, wrows, seps, per_shard
    )
    updated_far = to_core(updated, line)

    both = jnp.stack(
        [
            jnp.where(c == 0, updated, updated_far).reshape(2, SIDES, rows, width),
            jnp.where(c == 0, updated_far, updated).reshape(2, SIDES, rows, width),
        ],
        axis=2,
    ).reshape(2 * QUAD * rows, width)

    def block(part):
        return (-contract_last(part, both)).astype(jnp.bfloat16)

    results = {0: block(wrows)}
    up = down = wrows
    for s in range(1, line):
        if 2 * s < line:
            up = hop(up, line, 1, s - 1, line - 2)
            down = hop(down, line, -1, 1, line - s)
            results[s] = hop(block(up), line, -s, s, line - 1)
            results[-s] = hop(block(down), line, s, 0, line - 1 - s)
            continue
        if 2 * (s - 1) < line:
            up = hop(up, line, 1, s - 1, line - 2)
            down = hop(down, line, -1, 1, line - s)
            one = jnp.where(z >= s, up, down)
        else:
            last = s

            def outward(zz, yy, cc):
                if last - 1 <= zz < line - 1:
                    return (zz + 1, yy, cc)
                if 1 <= zz <= line - last:
                    return (zz - 1, yy, cc)
                return None

            one = sent(one, line, outward)
        span = s

        def home(zz, yy, cc):
            if zz >= span:
                return (zz - span, yy, cc)
            if zz + span < line:
                return (zz + span, yy, cc)
            return None

        results[s] = results[-s] = sent(block(one), line, home)

    quads = []
    for q in range(line):
        piece = results[0]
        for d in range(-q, line - q):
            if d:
                piece = jnp.where(z == q + d, results[-d], piece)
        quads.append(piece.reshape(rows, 2, QUAD * rows))
    rounded = jnp.stack(quads, axis=2).reshape(rows, 2 * width)
    sigma = rounded.astype(jnp.float32)

    if rows < TILE:
        whole = factor
        for bit in range((TILE // rows).bit_length() - 1):
            pairs = [(i, i ^ 1 << bit) for i in range(lax.axis_size("rows"))]
            partner = lax.ppermute(whole, "rows", pairs)
            whole = jnp.where(
                index >> bit & 1 == 0,
                jnp.concatenate([whole, partner], axis=0),
                jnp.concatenate([partner, whole], axis=0),
            )
        product = contract_last(rounded, whole)
        start = index * rows // TILE * TILE
        wtile = lax.dynamic_slice_in_dim(wrows, start, TILE, 1).astype(jnp.float32)
        result_tiles = wtile - product
    else:
        many = rows // TILE
        product = jnp.einsum(
            "mrk,mck->mrc",
            rounded.reshape(many, TILE, 2 * width),
            factor.reshape(many, TILE, 2 * width),
            preferred_element_type=jnp.float32,
        )
        square = lax.dynamic_slice_in_dim(wrows, index * rows, rows, 1).reshape(
            many, TILE, many, TILE
        )
        wtile = jnp.stack([square[i, :, i, :] for i in range(many)]).astype(jnp.float32)
        result_tiles = (wtile - product).reshape(rows, TILE)
    return (sigma[None], result_tiles[None])


def solution(mesh):
    placed = (
        P("tm", "rows", None),
        P("tm", "rows", None, None),
        P("tm", "rows", None),
        P("tm", "rows", None),
        P("tm", "rows", None),
    )
    return jax.shard_map(
        functools.partial(shards, mesh.shape["rows"] // QUAD),
        mesh=mesh,
        in_specs=placed,
        out_specs=(P("tm", "rows", None), P("tm", "rows", None)),
        check_vma=False,
    )
```

```python
import functools

import jax
import jax.numpy as jnp
from jax import lax
from jax.experimental import pallas as pl
from jax.experimental.pallas import tpu as pltpu
from jax.sharding import PartitionSpec as P

TILE = 128
PAD = 32
SIDES = 2
CORES = 2

WHOLE = pl.BlockSpec(memory_space=pltpu.VMEM)
SCALAR = pl.BlockSpec(memory_space=pltpu.SMEM)


def contract_last(left, right):
    return lax.dot_general(
        left, right, (((1,), (1,)), ((), ())), preferred_element_type=jnp.float32
    )


class Ring:
    def __init__(self, devices):
        self.line = devices // (SIDES * CORES)
        self.count = self.line * SIDES
        ups = [(z, 0) for z in range(self.line)]
        downs = [(z, 1) for z in reversed(range(self.line))]
        self.chips = [z * SIDES + y for z, y in ups + downs]
        self.spots = [self.chips.index(chip) for chip in range(self.count)]

    def turn(self, part, by):
        pairs = []
        for at, chip in enumerate(self.chips):
            target = self.chips[(at + by) % self.count]
            pairs += [(chip * CORES + c, target * CORES + c) for c in range(CORES)]
        return lax.ppermute(part, "rows", pairs)

    def to_core(self, part):
        devices = self.count * CORES
        return lax.ppermute(part, "rows", [(i, i ^ 1) for i in range(devices)])

    def opposite(self, ahead, behind):
        half = ahead.shape[0] // 2
        first = self.turn(ahead[:half], 1)
        return jnp.concatenate([first, self.turn(behind[half:], -1)], axis=0)


def pack_kernel(pos_ref, tiles_ref, cross_ref, packed_ref, flipped_ref):
    count = tiles_ref.shape[0]
    packed_ref[: count * TILE, :] = tiles_ref[...].reshape(count * TILE, TILE)
    lane = lax.broadcasted_iota(jnp.int32, (PAD, TILE), 1)
    marks = jnp.zeros((PAD, TILE), jnp.int32)
    for k in range(2 * count):
        marks = jnp.where(lane == k, pos_ref[k // 2, k % 2], marks)
    packed_ref[count * TILE :, :] = marks.astype(jnp.float32).astype(jnp.bfloat16)
    flipped_ref[...] = cross_ref[...].T


def pack(tiles, positions, cross):
    rows, width = cross.shape
    return pl.pallas_call(
        pack_kernel,
        out_shape=(
            jax.ShapeDtypeStruct((tiles.shape[0] * TILE + PAD, TILE), jnp.bfloat16),
            jax.ShapeDtypeStruct((width, rows), jnp.bfloat16),
        ),
        in_specs=[SCALAR, WHOLE, WHOLE],
        out_specs=(WHOLE, WHOLE),
        compiler_params=pltpu.CompilerParams(vmem_limit_bytes=16 * 1024 * 1024),
        cost_estimate=pl.CostEstimate(flops=0, bytes_accessed=rows, transcendentals=0),
    )(positions, tiles, cross)


def factors_kernel(
    per_shard,
    shards_each,
    near_ref,
    far_ref,
    wrows_ref,
    diag_ref,
    cross_ref,
    cols_ref,
    next_ref,
    updated_ref,
    factor_ref,
    sep_ref,
    wtile_ref,
    sum_ref,
    fac_ref,
    marks_ref,
    pos_ref,
    pos_sem,
):
    rows = wrows_ref.shape[0]
    count = wrows_ref.shape[1] // TILE
    stride = per_shard * TILE + PAD
    for half, ref in enumerate((near_ref, far_ref)):
        for s in range(shards_each):
            row = ref[s * stride + per_shard * TILE : (s + 1) * stride, :]
            marks_ref[half * shards_each + s] = row.astype(jnp.float32).astype(jnp.int32)[:8]
    fetch = pltpu.make_async_copy(marks_ref, pos_ref, pos_sem)
    fetch.start()
    for j in range(count):
        lanes = slice(j * TILE, (j + 1) * TILE)
        sep_ref[j, :rows, :] = diag_ref[:, lanes]
        sep_ref[j, rows:, :] = cols_ref[:, lanes]
        sep_ref[count + j, :rows, :] = cross_ref[:, lanes]
        sep_ref[count + j, rows:, :] = next_ref[:, lanes]
        wtile_ref[j] = wrows_ref[:, lanes]
    sum_ref[...] = jnp.zeros_like(sum_ref)
    fac_ref[...] = jnp.zeros_like(fac_ref)
    fetch.wait()

    def add(tile, shard, t):
        i = pos_ref[shard, 0, 2 * t]
        j = pos_ref[shard, 0, 2 * t + 1]
        sum_ref[i] += contract_last(sep_ref[j], tile)
        fac_ref[j] += jnp.dot(wtile_ref[i], tile, preferred_element_type=jnp.float32)

    @pl.loop(0, shards_each)
    def _(s):
        for half, ref in enumerate((near_ref, far_ref)):
            for t in range(per_shard):
                start = pl.multiple_of(s * stride + t * TILE, 16)
                add(ref[pl.ds(start, TILE), :], half * shards_each + s, t)

    for i in range(count):
        updated_ref[:, i * TILE : (i + 1) * TILE] = sum_ref[i].astype(jnp.bfloat16)
    for j in range(2 * count):
        factor_ref[:, j * TILE : (j + 1) * TILE] = fac_ref[j].astype(jnp.bfloat16)


def factors(near, far, wrows, seps, per_shard):
    rows, width = wrows.shape
    count = width // TILE
    shards_each = near.shape[0] // (per_shard * TILE + PAD)
    return pl.pallas_call(
        functools.partial(factors_kernel, per_shard, shards_each),
        out_shape=(
            jax.ShapeDtypeStruct((2 * rows, width), jnp.bfloat16),
            jax.ShapeDtypeStruct((rows, 2 * width), jnp.bfloat16),
        ),
        in_specs=[WHOLE] * (3 + len(seps)),
        out_specs=(WHOLE, WHOLE),
        scratch_shapes=[
            pltpu.VMEM((2 * count, 2 * rows, TILE), jnp.bfloat16),
            pltpu.VMEM((count, rows, TILE), jnp.bfloat16),
            pltpu.VMEM((count, 2 * rows, TILE), jnp.float32),
            pltpu.VMEM((2 * count, rows, TILE), jnp.float32),
            pltpu.VMEM((2 * shards_each, 8, TILE), jnp.int32),
            pltpu.SMEM((2 * shards_each, 8, TILE), jnp.int32),
            pltpu.SemaphoreType.DMA,
        ],
        compiler_params=pltpu.CompilerParams(vmem_limit_bytes=40 * 1024 * 1024),
        cost_estimate=pl.CostEstimate(flops=0, bytes_accessed=rows, transcendentals=0),
    )(near, far, wrows, *seps)


def products_kernel(many, *refs):
    lefts, (near_ref, far_ref), outs = refs[:many], refs[many : many + 2], refs[many + 2 :]
    size = near_ref.shape[0]
    for left_ref, out_ref in zip(lefts, outs):
        for at, ref in ((0, near_ref), (size, far_ref)):
            value = contract_last(left_ref[...], ref[...])
            out_ref[:, at : at + size] = (-value).astype(jnp.bfloat16)


def products(lefts, near, far):
    size = 2 * near.shape[0]
    return pl.pallas_call(
        functools.partial(products_kernel, len(lefts)),
        out_shape=tuple(jax.ShapeDtypeStruct((p.shape[0], size), jnp.bfloat16) for p in lefts),
        in_specs=[WHOLE] * (len(lefts) + 2),
        out_specs=(WHOLE,) * len(lefts),
        compiler_params=pltpu.CompilerParams(vmem_limit_bytes=32 * 1024 * 1024),
        cost_estimate=pl.CostEstimate(flops=0, bytes_accessed=size, transcendentals=0),
    )(*lefts, near, far)


def finish_kernel(line, place_ref, *refs):
    blocks = refs[: line * SIDES]
    factor_ref, wtile_ref, sigma_ref, tiles_ref = refs[line * SIDES :]
    rows = factor_ref.shape[0]
    width = sigma_ref.shape[1] // 2
    spot, core = place_ref[0], place_ref[1]
    total = wtile_ref[...].astype(jnp.float32)
    for d, ref in enumerate(blocks):
        at = lax.rem(spot + d, line * SIDES)
        chip = jnp.where(at < line, at * SIDES, (2 * line - 1 - at) * SIDES + 1)
        for turn in range(CORES):
            owner = core if turn == 0 else 1 - core
            for half in range(2):
                lane = (chip * CORES + owner) * rows + half * width
                lanes = pl.ds(pl.multiple_of(lane, TILE), rows)
                group = turn * 2 + half
                part = ref[:, group * rows : (group + 1) * rows]
                sigma_ref[:, lanes] = part.astype(jnp.float32)
                total -= contract_last(part, factor_ref[:, lanes])
    tiles_ref[...] = total


def finish(place, blocks, factor, wtile):
    rows = factor.shape[0]
    return pl.pallas_call(
        functools.partial(finish_kernel, len(blocks) // SIDES),
        out_shape=(
            jax.ShapeDtypeStruct(factor.shape, jnp.float32),
            jax.ShapeDtypeStruct((rows, TILE), jnp.float32),
        ),
        in_specs=[SCALAR] + [WHOLE] * (len(blocks) + 2),
        out_specs=(WHOLE, WHOLE),
        compiler_params=pltpu.CompilerParams(vmem_limit_bytes=24 * 1024 * 1024),
        cost_estimate=pl.CostEstimate(flops=0, bytes_accessed=rows, transcendentals=0),
    )(place, *blocks, factor, wtile)


def shards(ring, inverse_block, coupling_tiles, tile_pos, sep_diag, sep_cross):
    wrows = inverse_block[0]
    rows, width = wrows.shape
    tiles = coupling_tiles[0]
    per_shard = tiles.shape[0]
    diag = sep_diag[0]
    cross = sep_cross[0]
    index = lax.axis_index("rows")
    core = index % CORES
    spot = jnp.asarray(ring.spots, jnp.int32)[index // CORES]

    size = lax.axis_size("tm")
    following = lax.ppermute(diag, "tm", [(i + 1, i) for i in range(size - 1)])
    steps = ring.count // 2
    wahead = [wrows, ring.turn(wrows, 1)]
    wbehind = [wrows, ring.turn(wrows, -1)]
    packed, flipped = pack(tiles, tile_pos[0], cross)
    ahead, behind = ring.turn(packed, 1), ring.turn(packed, -1)
    ahead, behind, flipped = lax.optimization_barrier((ahead, behind, flipped))
    cols = lax.all_to_all(flipped, "rows", 0, 1, tiled=True)
    pieces = [packed, ahead, behind]
    for step in range(2, steps):
        ahead, behind = ring.turn(ahead, 1), ring.turn(behind, -1)
        if step == 2:
            ahead, behind, wahead[1], wbehind[1], following = lax.optimization_barrier(
                (ahead, behind, wahead[1], wbehind[1], following)
            )
        pieces += [ahead, behind]
    pieces.append(ring.opposite(ahead, behind))
    near = jnp.concatenate(pieces, axis=0)
    far = ring.to_core(near)

    updated, factor = factors(near, far, wrows, (diag, cross, cols, following), per_shard)
    for step in range(2, steps):
        wahead.append(ring.turn(wahead[-1], 1))
        wbehind.append(ring.turn(wbehind[-1], -1))
        if step == 2:
            updated, wahead[2], wbehind[2] = lax.optimization_barrier(
                (updated, wahead[2], wbehind[2])
            )
    other = ring.to_core(updated)

    early = min(3, steps)
    lefts = [wrows]
    for step in range(1, early):
        lefts += [wahead[step], wbehind[step]]
    done = products(lefts, updated, other)
    *done, wahead[-1], wbehind[-1] = lax.optimization_barrier((*done, wahead[-1], wbehind[-1]))
    last = ring.opposite(wahead[-1], wbehind[-1])
    blocks = [done[0]] + [None] * (ring.count - 1)
    for step in range(1, steps):
        if step < early:
            pair = done[2 * step - 1 : 2 * step + 1]
        else:
            pair = products([wahead[step], wbehind[step]], updated, other)
        blocks[step] = ring.turn(pair[0], -step)
        blocks[-step] = ring.turn(pair[1], step)
        if step == 1:
            last, blocks[1], blocks[-1] = lax.optimization_barrier((last, blocks[1], blocks[-1]))
    blocks[steps] = ring.turn(products([last], updated, other)[0], steps)

    if rows == TILE:
        wtile = lax.dynamic_slice_in_dim(wrows, index * rows, rows, 1)
        place = jnp.stack([spot, core]).astype(jnp.int32)
        sigma, result = finish(place, blocks, factor, wtile)
        return (sigma[None], result[None])
    order = (jnp.asarray(ring.spots, jnp.int32) - spot) % ring.count
    parts = jnp.take(jnp.stack(blocks), order, axis=0)
    parts = parts.reshape(ring.count, rows, CORES, 2, rows)
    parts = jnp.where(core == 0, parts, parts[:, :, ::-1])
    rounded = parts.transpose(1, 3, 0, 2, 4).reshape(rows, 2 * width)
    sigma = rounded.astype(jnp.float32)
    if rows < TILE:
        whole = factor
        for bit in range((TILE // rows).bit_length() - 1):
            pairs = [(i, i ^ 1 << bit) for i in range(lax.axis_size("rows"))]
            partner = lax.ppermute(whole, "rows", pairs)
            whole = jnp.where(
                index >> bit & 1 == 0,
                jnp.concatenate([whole, partner], axis=0),
                jnp.concatenate([partner, whole], axis=0),
            )
        overlap = contract_last(rounded, whole)
        start = index * rows // TILE * TILE
        wtile = lax.dynamic_slice_in_dim(wrows, start, TILE, 1).astype(jnp.float32)
        result_tiles = wtile - overlap
    else:
        many = rows // TILE
        overlap = jnp.einsum(
            "mrk,mck->mrc",
            rounded.reshape(many, TILE, 2 * width),
            factor.reshape(many, TILE, 2 * width),
            preferred_element_type=jnp.float32,
        )
        square = lax.dynamic_slice_in_dim(wrows, index * rows, rows, 1).reshape(
            many, TILE, many, TILE
        )
        wtile = jnp.stack([square[i, :, i, :] for i in range(many)]).astype(jnp.float32)
        result_tiles = (wtile - overlap).reshape(rows, TILE)
    return (sigma[None], result_tiles[None])


def solution(mesh):
    placed = (
        P("tm", "rows", None),
        P("tm", "rows", None, None),
        P("tm", "rows", None),
        P("tm", "rows", None),
        P("tm", "rows", None),
    )
    return jax.shard_map(
        functools.partial(shards, Ring(mesh.shape["rows"])),
        mesh=mesh,
        in_specs=placed,
        out_specs=(P("tm", "rows", None), P("tm", "rows", None)),
        check_vma=False,
    )
```

```python
import functools

import jax
import jax.numpy as jnp
from jax import lax
from jax.experimental import pallas as pl
from jax.experimental.pallas import tpu as pltpu
from jax.sharding import PartitionSpec as P

TILE = 128
PAD = 16
SIDES = 2
CORES = 2

WHOLE = pl.BlockSpec(memory_space=pltpu.VMEM)
SCALAR = pl.BlockSpec(memory_space=pltpu.SMEM)


def contract_last(left, right):
    return lax.dot_general(
        left, right, (((1,), (1,)), ((), ())), preferred_element_type=jnp.float32
    )


class Ring:
    def __init__(self, devices):
        self.line = devices // (SIDES * CORES)
        self.count = self.line * SIDES
        ups = [(z, 0) for z in range(self.line)]
        downs = [(z, 1) for z in reversed(range(self.line))]
        self.chips = [z * SIDES + y for z, y in ups + downs]
        self.spots = [self.chips.index(chip) for chip in range(self.count)]

    def turn(self, part, by):
        pairs = []
        for at, chip in enumerate(self.chips):
            target = self.chips[(at + by) % self.count]
            pairs += [(chip * CORES + c, target * CORES + c) for c in range(CORES)]
        return lax.ppermute(part, "rows", pairs)

    def to_core(self, part):
        devices = self.count * CORES
        return lax.ppermute(part, "rows", [(i, i ^ 1) for i in range(devices)])

    def opposite(self, ahead, behind):
        half = ahead.shape[0] // 2
        first = self.turn(ahead[:half], 1)
        return jnp.concatenate([first, self.turn(behind[half:], -1)], axis=0)


def flip_kernel(pos_ref, cross_ref, out_ref):
    devices, _, rows = out_ref.shape
    lane = lax.broadcasted_iota(jnp.int32, (PAD, rows), 1)
    marks = jnp.zeros((PAD, rows), jnp.int32)
    for k in range(pos_ref.shape[0]):
        marks = jnp.where(lane == 2 * k, pos_ref[k, 0], marks)
        marks = jnp.where(lane == 2 * k + 1, pos_ref[k, 1], marks)
    marks = marks.astype(jnp.float32).astype(jnp.bfloat16)
    for i in range(devices):
        out_ref[i, :rows, :] = cross_ref[:, i * rows : (i + 1) * rows].T
        out_ref[i, rows:, :] = marks


def flip(positions, cross):
    rows, width = cross.shape
    return pl.pallas_call(
        flip_kernel,
        out_shape=jax.ShapeDtypeStruct((width // rows, rows + PAD, rows), jnp.bfloat16),
        in_specs=[SCALAR, WHOLE],
        out_specs=WHOLE,
        compiler_params=pltpu.CompilerParams(vmem_limit_bytes=6 * 1024 * 1024),
        cost_estimate=pl.CostEstimate(flops=0, bytes_accessed=rows, transcendentals=0),
    )(positions, cross)


def read_marks(marks_in, first, marks_ref, pos_ref, pos_sem):
    devices, _, lanes = marks_in.shape
    for i in range(devices):
        row = marks_in[i, first : first + PAD, :].astype(jnp.float32).astype(jnp.int32)
        marks_ref[i, :, :lanes] = row[:8]
    fetch = pltpu.make_async_copy(marks_ref, pos_ref, pos_sem)
    fetch.start()
    return fetch


def each_tile(line, place_ref, near_ref, far_ref, pos_ref, add):
    spot, core = place_ref[0], place_ref[1]
    count = line * SIDES
    per_shard = near_ref.shape[0] // (count * TILE)

    @pl.loop(0, count)
    def _(s):
        step = (s + 1) // 2
        at = lax.rem(spot + jnp.where(s == 2 * step, step, count - step), count)
        chip = jnp.where(at < line, at * SIDES, (2 * line - 1 - at) * SIDES + 1)
        for turn, ref in enumerate((near_ref, far_ref)):
            source = chip * CORES + (core if turn == 0 else 1 - core)
            for t in range(per_shard):
                start = pl.multiple_of((s * per_shard + t) * TILE, TILE)
                tile = ref[pl.ds(start, TILE), :]
                add(tile, pos_ref[source, 0, 2 * t], pos_ref[source, 0, 2 * t + 1])


def mark_scratch(devices):
    return [
        pltpu.VMEM((devices, 8, TILE), jnp.int32),
        pltpu.SMEM((devices, 8, TILE), jnp.int32),
        pltpu.SemaphoreType.DMA,
    ]


def update_kernel(
    line,
    first,
    place_ref,
    near_ref,
    far_ref,
    marks_in,
    diag_ref,
    cross_ref,
    cols_ref,
    next_ref,
    out_ref,
    sep_ref,
    sum_ref,
    marks_ref,
    pos_ref,
    pos_sem,
):
    fetch = read_marks(marks_in, first, marks_ref, pos_ref, pos_sem)
    rows, width = diag_ref.shape
    count = width // TILE
    for j in range(count):
        lanes = slice(j * TILE, (j + 1) * TILE)
        sep_ref[j, :rows, :] = diag_ref[:, lanes]
        sep_ref[j, rows:, :] = cols_ref[j, :rows, :]
        sep_ref[count + j, :rows, :] = cross_ref[:, lanes]
        sep_ref[count + j, rows:, :] = next_ref[:, lanes]
    sum_ref[...] = jnp.zeros_like(sum_ref)
    fetch.wait()

    def add(tile, i, j):
        sum_ref[i] += contract_last(sep_ref[j], tile)

    each_tile(line, place_ref, near_ref, far_ref, pos_ref, add)
    for i in range(count):
        out_ref[:, i * TILE : (i + 1) * TILE] = sum_ref[i].astype(jnp.bfloat16)


def update(line, first, place, near, far, marks, diag, cross, cols, following):
    rows, width = diag.shape
    count = width // TILE
    return pl.pallas_call(
        functools.partial(update_kernel, line, first),
        out_shape=jax.ShapeDtypeStruct((2 * rows, width), jnp.bfloat16),
        in_specs=[SCALAR] + [WHOLE] * 7,
        out_specs=WHOLE,
        scratch_shapes=[
            pltpu.VMEM((2 * count, 2 * rows, TILE), jnp.bfloat16),
            pltpu.VMEM((count, 2 * rows, TILE), jnp.float32),
        ]
        + mark_scratch(marks.shape[0]),
        compiler_params=pltpu.CompilerParams(vmem_limit_bytes=12 * 1024 * 1024),
        cost_estimate=pl.CostEstimate(flops=0, bytes_accessed=rows, transcendentals=0),
    )(place, near, far, marks, diag, cross, cols, following)


def factor_kernel(
    line,
    first,
    place_ref,
    near_ref,
    far_ref,
    marks_in,
    wrows_ref,
    out_ref,
    wtile_ref,
    sum_ref,
    marks_ref,
    pos_ref,
    pos_sem,
):
    fetch = read_marks(marks_in, first, marks_ref, pos_ref, pos_sem)
    count = wrows_ref.shape[1] // TILE
    for j in range(count):
        wtile_ref[j] = wrows_ref[:, j * TILE : (j + 1) * TILE]
    sum_ref[...] = jnp.zeros_like(sum_ref)
    fetch.wait()

    def add(tile, i, j):
        sum_ref[j] += jnp.dot(wtile_ref[i], tile, preferred_element_type=jnp.float32)

    each_tile(line, place_ref, near_ref, far_ref, pos_ref, add)
    for j in range(2 * count):
        out_ref[:, j * TILE : (j + 1) * TILE] = sum_ref[j].astype(jnp.bfloat16)


def factor_rows(line, first, place, near, far, marks, wrows):
    rows, width = wrows.shape
    count = width // TILE
    return pl.pallas_call(
        functools.partial(factor_kernel, line, first),
        out_shape=jax.ShapeDtypeStruct((rows, 2 * width), jnp.bfloat16),
        in_specs=[SCALAR] + [WHOLE] * 4,
        out_specs=WHOLE,
        scratch_shapes=[
            pltpu.VMEM((count, rows, TILE), jnp.bfloat16),
            pltpu.VMEM((2 * count, rows, TILE), jnp.float32),
        ]
        + mark_scratch(marks.shape[0]),
        compiler_params=pltpu.CompilerParams(vmem_limit_bytes=8 * 1024 * 1024),
        cost_estimate=pl.CostEstimate(flops=0, bytes_accessed=rows, transcendentals=0),
    )(place, near, far, marks, wrows)


def products_kernel(many, *refs):
    lefts, (near_ref, far_ref), outs = refs[:many], refs[many : many + 2], refs[many + 2 : -1]
    all_ref = refs[-1]
    size = near_ref.shape[0]
    rows = lefts[0].shape[0]
    for k, left_ref in enumerate(lefts):
        all_ref[k * rows : (k + 1) * rows, :] = left_ref[...]
    for at, ref in ((0, near_ref), (size, far_ref)):
        value = (-contract_last(all_ref[...], ref[...])).astype(jnp.bfloat16)
        for k, out_ref in enumerate(outs):
            out_ref[:, at : at + size] = value[k * rows : (k + 1) * rows, :]


def products(lefts, near, far):
    size = 2 * near.shape[0]
    rows, width = lefts[0].shape
    return pl.pallas_call(
        functools.partial(products_kernel, len(lefts)),
        out_shape=(jax.ShapeDtypeStruct((rows, size), jnp.bfloat16),) * len(lefts),
        in_specs=[WHOLE] * (len(lefts) + 2),
        out_specs=(WHOLE,) * len(lefts),
        scratch_shapes=[pltpu.VMEM((len(lefts) * rows, width), jnp.bfloat16)],
        compiler_params=pltpu.CompilerParams(vmem_limit_bytes=12 * 1024 * 1024),
        cost_estimate=pl.CostEstimate(flops=0, bytes_accessed=size, transcendentals=0),
    )(*lefts, near, far)


def finish_kernel(line, place_ref, *refs):
    blocks = refs[: line * SIDES]
    factor_ref, wtile_ref, sigma_ref, tiles_ref = refs[line * SIDES :]
    rows = factor_ref.shape[0]
    width = sigma_ref.shape[1] // 2
    spot, core = place_ref[0], place_ref[1]
    total = wtile_ref[...].astype(jnp.float32)
    for d, ref in enumerate(blocks):
        at = lax.rem(spot + d, line * SIDES)
        chip = jnp.where(at < line, at * SIDES, (2 * line - 1 - at) * SIDES + 1)
        for turn in range(CORES):
            owner = core if turn == 0 else 1 - core
            for half in range(2):
                lane = (chip * CORES + owner) * rows + half * width
                lanes = pl.ds(pl.multiple_of(lane, TILE), rows)
                group = turn * 2 + half
                part = ref[:, group * rows : (group + 1) * rows]
                sigma_ref[:, lanes] = part.astype(jnp.float32)
                total -= contract_last(part, factor_ref[:, lanes])
    tiles_ref[...] = total


def finish(place, blocks, factor, wtile):
    rows = factor.shape[0]
    return pl.pallas_call(
        functools.partial(finish_kernel, len(blocks) // SIDES),
        out_shape=(
            jax.ShapeDtypeStruct(factor.shape, jnp.float32),
            jax.ShapeDtypeStruct((rows, TILE), jnp.float32),
        ),
        in_specs=[SCALAR] + [WHOLE] * (len(blocks) + 2),
        out_specs=(WHOLE, WHOLE),
        compiler_params=pltpu.CompilerParams(vmem_limit_bytes=10 * 1024 * 1024),
        cost_estimate=pl.CostEstimate(flops=0, bytes_accessed=rows, transcendentals=0),
    )(place, *blocks, factor, wtile)


def shards(ring, inverse_block, coupling_tiles, tile_pos, sep_diag, sep_cross):
    wrows = inverse_block[0]
    rows, width = wrows.shape
    tiles = coupling_tiles[0]
    per_shard = tiles.shape[0]
    diag = sep_diag[0]
    cross = sep_cross[0]
    index = lax.axis_index("rows")
    core = index % CORES
    chip = index // CORES
    far_side = chip % SIDES == 1
    spot = jnp.where(far_side, ring.count - 1 - chip // SIDES, chip // SIDES)

    place = jnp.stack([spot, core]).astype(jnp.int32)

    size = lax.axis_size("tm")
    steps = ring.count // 2
    plain = tiles.reshape(-1, TILE)
    wahead, wbehind = [wrows, ring.turn(wrows, 1)], [wrows, ring.turn(wrows, -1)]
    following = lax.ppermute(diag, "tm", [(i + 1, i) for i in range(size - 1)])
    flipped = flip(tile_pos[0], cross)
    pieces = [plain]
    ahead = behind = plain
    across = [ring.turn(plain, steps)]
    for step in range(1, steps - 0):
        ahead, behind = ring.turn(ahead, 1), ring.turn(behind, -1)
        beside = []
        if step == 1:
            across, ahead, behind = lax.optimization_barrier((across, ahead, behind))
        if step == 3:
            beside = [wahead[1], wbehind[1], following]
        if step == 1:
            ahead, behind, flipped, place, *beside = lax.optimization_barrier(
                (ahead, behind, flipped, place, *beside)
            )
            cols = lax.all_to_all(flipped, "rows", 0, 0, tiled=True)
        else:
            ahead, behind, *beside = lax.optimization_barrier((ahead, behind, *beside))
        if beside:
            wahead[1], wbehind[1], following = beside
        pieces += [ahead, behind]
    pieces += across[1:] + across[:1]
    for step in range(2, steps):
        wahead.append(ring.turn(wahead[-1], 1))
        wbehind.append(ring.turn(wbehind[-1], -1))
    near = jnp.concatenate(pieces, axis=0)
    if False:
        near, wahead[2], wbehind[2] = lax.optimization_barrier((near, wahead[2], wbehind[2]))
    far = ring.to_core(near)

    first, marks = rows, cols
    if rows < TILE:
        first, marks = 0, cols[:, rows:, :]
        cols = cols[:, :rows, :].reshape(width // TILE, TILE // rows, rows, rows)
        cols = cols.transpose(0, 2, 1, 3).reshape(width // TILE, rows, TILE)
    updated = update(ring.line, first, place, near, far, marks, diag, cross, cols, following)
    if not False:
        updated, wahead[2], wbehind[2] = lax.optimization_barrier(
            (updated, wahead[2], wbehind[2])
        )
    other = ring.to_core(updated)
    factor = factor_rows(ring.line, first, place, near, far, marks, wrows)

    early = min(3, steps)
    lefts = [wrows]
    for step in range(1, early):
        lefts += [wahead[step], wbehind[step]]
    done = products(lefts, updated, other)
    blocks = [done[0]] + [None] * (ring.count - 1)
    for step in range(1, early):
        blocks[step] = ring.turn(done[2 * step - 1], -step)
        blocks[-step] = ring.turn(done[2 * step], step)
        if step == 1:
            blocks[1], blocks[-1], wahead[-1], wbehind[-1] = lax.optimization_barrier(
                (blocks[1], blocks[-1], wahead[-1], wbehind[-1])
            )
    last = ring.opposite(wahead[-1], wbehind[-1])
    for step in range(early, steps):
        pair = products([wahead[step], wbehind[step]], updated, other)
        blocks[step] = ring.turn(pair[0], -step)
        blocks[-step] = ring.turn(pair[1], step)
    blocks[steps] = ring.turn(products([last], updated, other)[0], steps)

    if rows == TILE:
        wtile = lax.dynamic_slice_in_dim(wrows, index * rows, rows, 1)
        sigma, result = finish(place, blocks, factor, wtile)
        return (sigma[None], result[None])
    order = (jnp.asarray(ring.spots, jnp.int32) - spot) % ring.count
    parts = jnp.take(jnp.stack(blocks), order, axis=0)
    parts = parts.reshape(ring.count, rows, CORES, 2, rows)
    parts = jnp.where(core == 0, parts, parts[:, :, ::-1])
    rounded = parts.transpose(1, 3, 0, 2, 4).reshape(rows, 2 * width)
    sigma = rounded.astype(jnp.float32)
    if rows < TILE:
        whole = factor
        for bit in range((TILE // rows).bit_length() - 1):
            pairs = [(i, i ^ 1 << bit) for i in range(lax.axis_size("rows"))]
            partner = lax.ppermute(whole, "rows", pairs)
            whole = jnp.where(
                index >> bit & 1 == 0,
                jnp.concatenate([whole, partner], axis=0),
                jnp.concatenate([partner, whole], axis=0),
            )
        overlap = contract_last(rounded, whole)
        start = index * rows // TILE * TILE
        wtile = lax.dynamic_slice_in_dim(wrows, start, TILE, 1).astype(jnp.float32)
        result_tiles = wtile - overlap
    else:
        many = rows // TILE
        overlap = jnp.einsum(
            "mrk,mck->mrc",
            rounded.reshape(many, TILE, 2 * width),
            factor.reshape(many, TILE, 2 * width),
            preferred_element_type=jnp.float32,
        )
        square = lax.dynamic_slice_in_dim(wrows, index * rows, rows, 1).reshape(
            many, TILE, many, TILE
        )
        wtile = jnp.stack([square[i, :, i, :] for i in range(many)]).astype(jnp.float32)
        result_tiles = (wtile - overlap).reshape(rows, TILE)
    return (sigma[None], result_tiles[None])


def solution(mesh):
    placed = (
        P("tm", "rows", None),
        P("tm", "rows", None, None),
        P("tm", "rows", None),
        P("tm", "rows", None),
        P("tm", "rows", None),
    )
    return jax.shard_map(
        functools.partial(shards, Ring(mesh.shape["rows"])),
        mesh=mesh,
        in_specs=placed,
        out_specs=(P("tm", "rows", None), P("tm", "rows", None)),
        check_vma=False,
    )
```

```python
import functools

import jax
import jax.numpy as jnp
from jax import lax
from jax.experimental import pallas as pl
from jax.experimental.pallas import tpu as pltpu
from jax.sharding import PartitionSpec as P

TILE = 128
PAD = 16
SIDES = 2
CORES = 2

WHOLE = pl.BlockSpec(memory_space=pltpu.VMEM)
SCALAR = pl.BlockSpec(memory_space=pltpu.SMEM)
ANY = pl.BlockSpec(memory_space=pl.ANY)


def contract_last(left, right):
    return lax.dot_general(
        left, right, (((1,), (1,)), ((), ())), preferred_element_type=jnp.float32
    )


class Ring:
    def __init__(self, devices):
        self.line = devices // (SIDES * CORES)
        self.count = self.line * SIDES
        ups = [(z, 0) for z in range(self.line)]
        downs = [(z, 1) for z in reversed(range(self.line))]
        self.chips = [z * SIDES + y for z, y in ups + downs]
        self.spots = [self.chips.index(chip) for chip in range(self.count)]

    def turn(self, part, by):
        pairs = []
        for at, chip in enumerate(self.chips):
            target = self.chips[(at + by) % self.count]
            pairs += [(chip * CORES + c, target * CORES + c) for c in range(CORES)]
        return lax.ppermute(part, "rows", pairs)

    def to_core(self, part):
        devices = self.count * CORES
        return lax.ppermute(part, "rows", [(i, i ^ 1) for i in range(devices)])

    def opposite(self, ahead, behind):
        half = ahead.shape[0] // 2
        first = self.turn(ahead[:half], 1)
        return jnp.concatenate([first, self.turn(behind[half:], -1)], axis=0)


def flip_kernel(pos_ref, cross_ref, out_ref):
    devices, _, rows = out_ref.shape
    lane = lax.broadcasted_iota(jnp.int32, (PAD, rows), 1)
    marks = jnp.zeros((PAD, rows), jnp.int32)
    for k in range(pos_ref.shape[0]):
        marks = jnp.where(lane == 2 * k, pos_ref[k, 0], marks)
        marks = jnp.where(lane == 2 * k + 1, pos_ref[k, 1], marks)
    marks = marks.astype(jnp.float32).astype(jnp.bfloat16)
    for i in range(devices):
        out_ref[i, :rows, :] = cross_ref[:, i * rows : (i + 1) * rows].T
        out_ref[i, rows:, :] = marks


def flip(positions, cross):
    rows, width = cross.shape
    return pl.pallas_call(
        flip_kernel,
        out_shape=jax.ShapeDtypeStruct((width // rows, rows + PAD, rows), jnp.bfloat16),
        in_specs=[SCALAR, WHOLE],
        out_specs=WHOLE,
        compiler_params=pltpu.CompilerParams(vmem_limit_bytes=6 * 1024 * 1024),
        cost_estimate=pl.CostEstimate(flops=0, bytes_accessed=rows, transcendentals=0),
    )(positions, cross)


def read_marks(marks_in, first, marks_ref, pos_ref, pos_sem):
    devices, _, lanes = marks_in.shape
    for i in range(devices):
        row = marks_in[i, first : first + PAD, :].astype(jnp.float32).astype(jnp.int32)
        marks_ref[i, :, :lanes] = row[:8]
    fetch = pltpu.make_async_copy(marks_ref, pos_ref, pos_sem)
    fetch.start()
    return fetch


def each_tile(line, place_ref, near_ref, far_ref, pos_ref, add):
    spot, core = place_ref[0], place_ref[1]
    count = line * SIDES
    per_shard = near_ref.shape[0] // (count * TILE)

    @pl.loop(0, count)
    def _(s):
        step = (s + 1) // 2
        at = lax.rem(spot + jnp.where(s == 2 * step, step, count - step), count)
        chip = jnp.where(at < line, at * SIDES, (2 * line - 1 - at) * SIDES + 1)
        for turn, ref in enumerate((near_ref, far_ref)):
            source = chip * CORES + (core if turn == 0 else 1 - core)
            for t in range(per_shard):
                start = pl.multiple_of((s * per_shard + t) * TILE, TILE)
                tile = ref[pl.ds(start, TILE), :]
                add(tile, pos_ref[source, 0, 2 * t], pos_ref[source, 0, 2 * t + 1])


def mark_scratch(devices):
    return [
        pltpu.VMEM((devices, 8, TILE), jnp.int32),
        pltpu.SMEM((devices, 8, TILE), jnp.int32),
        pltpu.SemaphoreType.DMA,
    ]


def update_kernel(
    line,
    first,
    place_ref,
    near_ref,
    far_ref,
    marks_in,
    diag_in,
    cross_in,
    cols_ref,
    next_in,
    out_ref,
    sep_ref,
    sum_ref,
    loaded_ref,
    sems,
    marks_ref,
    pos_ref,
    pos_sem,
):
    loads = []
    for k, source in enumerate((diag_in, cross_in, next_in)):
        loads.append(pltpu.make_async_copy(source, loaded_ref.at[k], sems.at[k]))
        loads[-1].start()
    fetch = read_marks(marks_in, first, marks_ref, pos_ref, pos_sem)
    sum_ref[...] = jnp.zeros_like(sum_ref)
    for load in loads:
        load.wait()
    _, rows, width = loaded_ref.shape
    count = width // TILE
    for j in range(count):
        lanes = slice(j * TILE, (j + 1) * TILE)
        sep_ref[j, :rows, :] = loaded_ref[0, :, lanes]
        sep_ref[j, rows:, :] = cols_ref[j, :rows, :]
        sep_ref[count + j, :rows, :] = loaded_ref[1, :, lanes]
        sep_ref[count + j, rows:, :] = loaded_ref[2, :, lanes]
    fetch.wait()

    def add(tile, i, j):
        sum_ref[i] += contract_last(sep_ref[j], tile)

    each_tile(line, place_ref, near_ref, far_ref, pos_ref, add)
    for i in range(count):
        out_ref[:, i * TILE : (i + 1) * TILE] = sum_ref[i].astype(jnp.bfloat16)


def update(line, first, place, near, far, marks, diag, cross, cols, following):
    rows, width = diag.shape
    count = width // TILE
    return pl.pallas_call(
        functools.partial(update_kernel, line, first),
        out_shape=jax.ShapeDtypeStruct((2 * rows, width), jnp.bfloat16),
        in_specs=[SCALAR] + [WHOLE] * 3 + [ANY, ANY, WHOLE, ANY],
        out_specs=WHOLE,
        scratch_shapes=[
            pltpu.VMEM((2 * count, 2 * rows, TILE), jnp.bfloat16),
            pltpu.VMEM((count, 2 * rows, TILE), jnp.float32),
            pltpu.VMEM((3, rows, width), jnp.bfloat16),
            pltpu.SemaphoreType.DMA((3,)),
        ]
        + mark_scratch(marks.shape[0]),
        compiler_params=pltpu.CompilerParams(vmem_limit_bytes=54 * 1024 * 1024),
        cost_estimate=pl.CostEstimate(flops=0, bytes_accessed=rows, transcendentals=0),
    )(place, near, far, marks, diag, cross, cols, following)


def factor_kernel(
    line,
    first,
    place_ref,
    near_ref,
    far_ref,
    marks_in,
    wrows_ref,
    out_ref,
    wtile_ref,
    sum_ref,
    marks_ref,
    pos_ref,
    pos_sem,
):
    fetch = read_marks(marks_in, first, marks_ref, pos_ref, pos_sem)
    count = wrows_ref.shape[1] // TILE
    for j in range(count):
        wtile_ref[j] = wrows_ref[:, j * TILE : (j + 1) * TILE]
    sum_ref[...] = jnp.zeros_like(sum_ref)
    fetch.wait()

    def add(tile, i, j):
        sum_ref[j] += jnp.dot(wtile_ref[i], tile, preferred_element_type=jnp.float32)

    each_tile(line, place_ref, near_ref, far_ref, pos_ref, add)
    for j in range(2 * count):
        out_ref[:, j * TILE : (j + 1) * TILE] = sum_ref[j].astype(jnp.bfloat16)


def factor_rows(line, first, place, near, far, marks, wrows):
    rows, width = wrows.shape
    count = width // TILE
    return pl.pallas_call(
        functools.partial(factor_kernel, line, first),
        out_shape=jax.ShapeDtypeStruct((rows, 2 * width), jnp.bfloat16),
        in_specs=[SCALAR] + [WHOLE] * 4,
        out_specs=WHOLE,
        scratch_shapes=[
            pltpu.VMEM((count, rows, TILE), jnp.bfloat16),
            pltpu.VMEM((2 * count, rows, TILE), jnp.float32),
        ]
        + mark_scratch(marks.shape[0]),
        compiler_params=pltpu.CompilerParams(vmem_limit_bytes=8 * 1024 * 1024),
        cost_estimate=pl.CostEstimate(flops=0, bytes_accessed=rows, transcendentals=0),
    )(place, near, far, marks, wrows)


def products_kernel(many, *refs):
    lefts, (near_ref, far_ref), outs = refs[:many], refs[many : many + 2], refs[many + 2 : -1]
    all_ref = refs[-1]
    size = near_ref.shape[0]
    rows = lefts[0].shape[0]
    for k, left_ref in enumerate(lefts):
        all_ref[k * rows : (k + 1) * rows, :] = left_ref[...]
    for at, ref in ((0, near_ref), (size, far_ref)):
        value = (-contract_last(all_ref[...], ref[...])).astype(jnp.bfloat16)
        for k, out_ref in enumerate(outs):
            out_ref[:, at : at + size] = value[k * rows : (k + 1) * rows, :]


def products(lefts, near, far):
    size = 2 * near.shape[0]
    rows, width = lefts[0].shape
    return pl.pallas_call(
        functools.partial(products_kernel, len(lefts)),
        out_shape=(jax.ShapeDtypeStruct((rows, size), jnp.bfloat16),) * len(lefts),
        in_specs=[WHOLE] * (len(lefts) + 2),
        out_specs=(WHOLE,) * len(lefts),
        scratch_shapes=[pltpu.VMEM((len(lefts) * rows, width), jnp.bfloat16)],
        compiler_params=pltpu.CompilerParams(vmem_limit_bytes=12 * 1024 * 1024),
        cost_estimate=pl.CostEstimate(flops=0, bytes_accessed=size, transcendentals=0),
    )(*lefts, near, far)


def finish_kernel(line, place_ref, *refs):
    blocks = refs[: line * SIDES]
    factor_ref, wtile_ref, sigma_ref, tiles_ref = refs[line * SIDES :]
    rows = factor_ref.shape[0]
    width = sigma_ref.shape[1] // 2
    spot, core = place_ref[0], place_ref[1]
    total = wtile_ref[...].astype(jnp.float32)
    for d, ref in enumerate(blocks):
        at = lax.rem(spot + d, line * SIDES)
        chip = jnp.where(at < line, at * SIDES, (2 * line - 1 - at) * SIDES + 1)
        for turn in range(CORES):
            owner = core if turn == 0 else 1 - core
            for half in range(2):
                lane = (chip * CORES + owner) * rows + half * width
                lanes = pl.ds(pl.multiple_of(lane, TILE), rows)
                group = turn * 2 + half
                part = ref[:, group * rows : (group + 1) * rows]
                sigma_ref[:, lanes] = part.astype(jnp.float32)
                total -= contract_last(part, factor_ref[:, lanes])
    tiles_ref[...] = total


def finish(place, blocks, factor, wtile):
    rows = factor.shape[0]
    return pl.pallas_call(
        functools.partial(finish_kernel, len(blocks) // SIDES),
        out_shape=(
            jax.ShapeDtypeStruct(factor.shape, jnp.float32),
            jax.ShapeDtypeStruct((rows, TILE), jnp.float32),
        ),
        in_specs=[SCALAR] + [WHOLE] * (len(blocks) + 2),
        out_specs=(WHOLE, WHOLE),
        compiler_params=pltpu.CompilerParams(vmem_limit_bytes=10 * 1024 * 1024),
        cost_estimate=pl.CostEstimate(flops=0, bytes_accessed=rows, transcendentals=0),
    )(place, *blocks, factor, wtile)


def shards(ring, inverse_block, coupling_tiles, tile_pos, sep_diag, sep_cross):
    wrows = inverse_block[0]
    rows, width = wrows.shape
    tiles = coupling_tiles[0]
    per_shard = tiles.shape[0]
    diag = sep_diag[0]
    cross = sep_cross[0]
    index = lax.axis_index("rows")
    core = index % CORES
    chip = index // CORES
    far_side = chip % SIDES == 1
    spot = jnp.where(far_side, ring.count - 1 - chip // SIDES, chip // SIDES)

    place = jnp.stack([spot, core]).astype(jnp.int32)

    size = lax.axis_size("tm")
    steps = ring.count // 2
    plain = tiles.reshape(-1, TILE)
    wahead, wbehind = [wrows, ring.turn(wrows, 1)], [wrows, ring.turn(wrows, -1)]
    second = [ring.turn(wahead[1], 1), ring.turn(wbehind[1], -1)]
    following = lax.ppermute(diag, "tm", [(i + 1, i) for i in range(size - 1)])
    flipped = flip(tile_pos[0], cross)
    pieces = [plain]
    ahead = behind = plain
    across = [ring.turn(plain, steps)]
    for step in range(1, steps - 0):
        ahead, behind = ring.turn(ahead, 1), ring.turn(behind, -1)
        beside = []
        if step == 1:
            across, ahead, behind = lax.optimization_barrier((across, ahead, behind))
        if step == 3:
            beside = [wahead[1], wbehind[1], following]
        if step == 1:
            ahead, behind, flipped, place, *beside = lax.optimization_barrier(
                (ahead, behind, flipped, place, *beside)
            )
            cols = lax.all_to_all(flipped, "rows", 0, 0, tiled=True)
        else:
            ahead, behind, *beside = lax.optimization_barrier((ahead, behind, *beside))
        if beside:
            wahead[1], wbehind[1], following = beside
        pieces += [ahead, behind]
    pieces += across[1:] + across[:1]
    wahead.append(second[0])
    wbehind.append(second[1])
    near = jnp.concatenate(pieces, axis=0)
    far = ring.to_core(near)

    first, marks = rows, cols
    if rows < TILE:
        first, marks = 0, cols[:, rows:, :]
        cols = cols[:, :rows, :].reshape(width // TILE, TILE // rows, rows, rows)
        cols = cols.transpose(0, 2, 1, 3).reshape(width // TILE, rows, TILE)
    updated = update(ring.line, first, place, near, far, marks, diag, cross, cols, following)
    updated, wahead[2], wbehind[2] = lax.optimization_barrier((updated, wahead[2], wbehind[2]))
    for step in range(3, steps):
        wahead.append(ring.turn(wahead[-1], 1))
        wbehind.append(ring.turn(wbehind[-1], -1))
    other = ring.to_core(updated)
    factor = factor_rows(ring.line, first, place, near, far, marks, wrows)

    early = min(3, steps)
    lefts = [wrows]
    for step in range(1, early):
        lefts += [wahead[step], wbehind[step]]
    done = products(lefts, updated, other)
    blocks = [done[0]] + [None] * (ring.count - 1)
    for step in range(1, early):
        blocks[step] = ring.turn(done[2 * step - 1], -step)
        blocks[-step] = ring.turn(done[2 * step], step)
        if step == 1:
            blocks[1], blocks[-1], wahead[-1], wbehind[-1] = lax.optimization_barrier(
                (blocks[1], blocks[-1], wahead[-1], wbehind[-1])
            )
    last = ring.opposite(wahead[-1], wbehind[-1])
    for step in range(early, steps):
        pair = products([wahead[step], wbehind[step]], updated, other)
        blocks[step] = ring.turn(pair[0], -step)
        blocks[-step] = ring.turn(pair[1], step)
    blocks[steps] = ring.turn(products([last], updated, other)[0], steps)

    if rows == TILE:
        wtile = lax.dynamic_slice_in_dim(wrows, index * rows, rows, 1)
        sigma, result = finish(place, blocks, factor, wtile)
        return (sigma[None], result[None])
    order = (jnp.asarray(ring.spots, jnp.int32) - spot) % ring.count
    parts = jnp.take(jnp.stack(blocks), order, axis=0)
    parts = parts.reshape(ring.count, rows, CORES, 2, rows)
    parts = jnp.where(core == 0, parts, parts[:, :, ::-1])
    rounded = parts.transpose(1, 3, 0, 2, 4).reshape(rows, 2 * width)
    sigma = rounded.astype(jnp.float32)
    if rows < TILE:
        whole = factor
        for bit in range((TILE // rows).bit_length() - 1):
            pairs = [(i, i ^ 1 << bit) for i in range(lax.axis_size("rows"))]
            partner = lax.ppermute(whole, "rows", pairs)
            whole = jnp.where(
                index >> bit & 1 == 0,
                jnp.concatenate([whole, partner], axis=0),
                jnp.concatenate([partner, whole], axis=0),
            )
        overlap = contract_last(rounded, whole)
        start = index * rows // TILE * TILE
        wtile = lax.dynamic_slice_in_dim(wrows, start, TILE, 1).astype(jnp.float32)
        result_tiles = wtile - overlap
    else:
        many = rows // TILE
        overlap = jnp.einsum(
            "mrk,mck->mrc",
            rounded.reshape(many, TILE, 2 * width),
            factor.reshape(many, TILE, 2 * width),
            preferred_element_type=jnp.float32,
        )
        square = lax.dynamic_slice_in_dim(wrows, index * rows, rows, 1).reshape(
            many, TILE, many, TILE
        )
        wtile = jnp.stack([square[i, :, i, :] for i in range(many)]).astype(jnp.float32)
        result_tiles = (wtile - overlap).reshape(rows, TILE)
    return (sigma[None], result_tiles[None])


def solution(mesh):
    placed = (
        P("tm", "rows", None),
        P("tm", "rows", None, None),
        P("tm", "rows", None),
        P("tm", "rows", None),
        P("tm", "rows", None),
    )
    return jax.shard_map(
        functools.partial(shards, Ring(mesh.shape["rows"])),
        mesh=mesh,
        in_specs=placed,
        out_specs=(P("tm", "rows", None), P("tm", "rows", None)),
        check_vma=False,
    )
```

```python
import functools

import jax
import jax.numpy as jnp
from jax import lax
from jax.experimental import pallas as pl
from jax.experimental.pallas import tpu as pltpu
from jax.sharding import PartitionSpec as P

TILE = 128
PAD = 16
SIDES = 2
CORES = 2

WHOLE = pl.BlockSpec(memory_space=pltpu.VMEM)
SCALAR = pl.BlockSpec(memory_space=pltpu.SMEM)
ANY = pl.BlockSpec(memory_space=pl.ANY)


def contract_last(left, right):
    return lax.dot_general(
        left, right, (((1,), (1,)), ((), ())), preferred_element_type=jnp.float32
    )


class Ring:
    def __init__(self, devices):
        self.line = devices // (SIDES * CORES)
        self.count = self.line * SIDES
        ups = [(z, 0) for z in range(self.line)]
        downs = [(z, 1) for z in reversed(range(self.line))]
        self.chips = [z * SIDES + y for z, y in ups + downs]
        self.spots = [self.chips.index(chip) for chip in range(self.count)]

    def turn(self, part, by):
        pairs = []
        for at, chip in enumerate(self.chips):
            target = self.chips[(at + by) % self.count]
            pairs += [(chip * CORES + c, target * CORES + c) for c in range(CORES)]
        return lax.ppermute(part, "rows", pairs)

    def move(self, part, by, cross=0):
        pairs = []
        for z in range(self.line):
            for y in range(SIDES):
                source = (z * SIDES + y) * CORES
                target = ((z + by) % self.line * SIDES + (y ^ cross)) * CORES
                pairs += [(source + c, target + c) for c in range(CORES)]
        return lax.ppermute(part, "rows", pairs)

    def to_core(self, part):
        devices = self.count * CORES
        return lax.ppermute(part, "rows", [(i, i ^ 1) for i in range(devices)])

    def opposite(self, ahead, behind):
        half = ahead.shape[0] // 2
        return [self.turn(ahead[:half], 1), self.turn(behind[half:], -1)]


def flip_kernel(pos_ref, cross_ref, out_ref):
    devices, _, rows = out_ref.shape
    lane = lax.broadcasted_iota(jnp.int32, (PAD, rows), 1)
    marks = jnp.zeros((PAD, rows), jnp.int32)
    for k in range(pos_ref.shape[0]):
        marks = jnp.where(lane == 2 * k, pos_ref[k, 0], marks)
        marks = jnp.where(lane == 2 * k + 1, pos_ref[k, 1], marks)
    marks = marks.astype(jnp.float32).astype(jnp.bfloat16)
    for i in range(devices):
        out_ref[i, :rows, :] = cross_ref[:, i * rows : (i + 1) * rows].T
        out_ref[i, rows:, :] = marks


def flip(positions, cross):
    rows, width = cross.shape
    return pl.pallas_call(
        flip_kernel,
        out_shape=jax.ShapeDtypeStruct((width // rows, rows + PAD, rows), jnp.bfloat16),
        in_specs=[SCALAR, WHOLE],
        out_specs=WHOLE,
        compiler_params=pltpu.CompilerParams(vmem_limit_bytes=6 * 1024 * 1024),
        cost_estimate=pl.CostEstimate(flops=0, bytes_accessed=rows, transcendentals=0),
    )(positions, cross)


def read_marks(marks_in, first, marks_ref, pos_ref, pos_sem):
    devices, _, lanes = marks_in.shape
    for i in range(devices):
        row = marks_in[i, first : first + PAD, :].astype(jnp.float32).astype(jnp.int32)
        marks_ref[i, :, :lanes] = row[:8]
    fetch = pltpu.make_async_copy(marks_ref, pos_ref, pos_sem)
    fetch.start()
    return fetch


def each_tile(line, place_ref, near_ref, far_ref, pos_ref, add):
    core = place_ref[1]
    count = line * SIDES
    per_shard = near_ref.shape[0] // (count * TILE)

    @pl.loop(0, count)
    def _(s):
        chip = place_ref[2 + s]
        for turn, ref in enumerate((near_ref, far_ref)):
            source = chip * CORES + (core if turn == 0 else 1 - core)
            for t in range(per_shard):
                start = pl.multiple_of((s * per_shard + t) * TILE, TILE)
                tile = ref[pl.ds(start, TILE), :]
                add(tile, pos_ref[source, 0, 2 * t], pos_ref[source, 0, 2 * t + 1])


def mark_scratch(devices):
    return [
        pltpu.VMEM((devices, 8, TILE), jnp.int32),
        pltpu.SMEM((devices, 8, TILE), jnp.int32),
        pltpu.SemaphoreType.DMA,
    ]


def update_kernel(
    line,
    first,
    place_ref,
    near_ref,
    far_ref,
    marks_in,
    diag_in,
    cross_in,
    cols_ref,
    next_in,
    out_ref,
    sep_ref,
    sum_ref,
    loaded_ref,
    sems,
    marks_ref,
    pos_ref,
    pos_sem,
):
    loads = []
    for k, source in enumerate((diag_in, cross_in, next_in)):
        loads.append(pltpu.make_async_copy(source, loaded_ref.at[k], sems.at[k]))
        loads[-1].start()
    fetch = read_marks(marks_in, first, marks_ref, pos_ref, pos_sem)
    sum_ref[...] = jnp.zeros_like(sum_ref)
    for load in loads:
        load.wait()
    _, rows, width = loaded_ref.shape
    count = width // TILE
    for j in range(count):
        lanes = slice(j * TILE, (j + 1) * TILE)
        sep_ref[j, :rows, :] = loaded_ref[0, :, lanes]
        sep_ref[j, rows:, :] = cols_ref[j, :rows, :]
        sep_ref[count + j, :rows, :] = loaded_ref[1, :, lanes]
        sep_ref[count + j, rows:, :] = loaded_ref[2, :, lanes]
    fetch.wait()

    def add(tile, i, j):
        sum_ref[i] += contract_last(sep_ref[j], tile)

    each_tile(line, place_ref, near_ref, far_ref, pos_ref, add)
    for i in range(count):
        out_ref[:, i * TILE : (i + 1) * TILE] = sum_ref[i].astype(jnp.bfloat16)


def update(line, first, place, near, far, marks, diag, cross, cols, following):
    rows, width = diag.shape
    count = width // TILE
    return pl.pallas_call(
        functools.partial(update_kernel, line, first),
        out_shape=jax.ShapeDtypeStruct((2 * rows, width), jnp.bfloat16),
        in_specs=[SCALAR] + [WHOLE] * 3 + [ANY, ANY, WHOLE, ANY],
        out_specs=WHOLE,
        scratch_shapes=[
            pltpu.VMEM((2 * count, 2 * rows, TILE), jnp.bfloat16),
            pltpu.VMEM((count, 2 * rows, TILE), jnp.float32),
            pltpu.VMEM((3, rows, width), jnp.bfloat16),
            pltpu.SemaphoreType.DMA((3,)),
        ]
        + mark_scratch(marks.shape[0]),
        compiler_params=pltpu.CompilerParams(vmem_limit_bytes=54 * 1024 * 1024),
        cost_estimate=pl.CostEstimate(flops=0, bytes_accessed=rows, transcendentals=0),
    )(place, near, far, marks, diag, cross, cols, following)


def factor_kernel(
    line,
    first,
    place_ref,
    near_ref,
    far_ref,
    marks_in,
    wrows_ref,
    out_ref,
    wtile_ref,
    sum_ref,
    marks_ref,
    pos_ref,
    pos_sem,
):
    fetch = read_marks(marks_in, first, marks_ref, pos_ref, pos_sem)
    count = wrows_ref.shape[1] // TILE
    for j in range(count):
        wtile_ref[j] = wrows_ref[:, j * TILE : (j + 1) * TILE]
    sum_ref[...] = jnp.zeros_like(sum_ref)
    fetch.wait()

    def add(tile, i, j):
        sum_ref[j] += jnp.dot(wtile_ref[i], tile, preferred_element_type=jnp.float32)

    each_tile(line, place_ref, near_ref, far_ref, pos_ref, add)
    for j in range(2 * count):
        out_ref[:, j * TILE : (j + 1) * TILE] = sum_ref[j].astype(jnp.bfloat16)


def factor_rows(line, first, place, near, far, marks, wrows):
    rows, width = wrows.shape
    count = width // TILE
    return pl.pallas_call(
        functools.partial(factor_kernel, line, first),
        out_shape=jax.ShapeDtypeStruct((rows, 2 * width), jnp.bfloat16),
        in_specs=[SCALAR] + [WHOLE] * 4,
        out_specs=WHOLE,
        scratch_shapes=[
            pltpu.VMEM((count, rows, TILE), jnp.bfloat16),
            pltpu.VMEM((2 * count, rows, TILE), jnp.float32),
        ]
        + mark_scratch(marks.shape[0]),
        compiler_params=pltpu.CompilerParams(vmem_limit_bytes=8 * 1024 * 1024),
        cost_estimate=pl.CostEstimate(flops=0, bytes_accessed=rows, transcendentals=0),
    )(place, near, far, marks, wrows)


def products_kernel(many, *refs):
    lefts, (near_ref, far_ref), outs = refs[:many], refs[many : many + 2], refs[many + 2 : -1]
    all_ref = refs[-1]
    size = near_ref.shape[0]
    at = 0
    for left_ref in lefts:
        all_ref[at : at + left_ref.shape[0], :] = left_ref[...]
        at += left_ref.shape[0]
    rows = outs[0].shape[0]
    for at, ref in ((0, near_ref), (size, far_ref)):
        value = (-contract_last(all_ref[...], ref[...])).astype(jnp.bfloat16)
        for k, out_ref in enumerate(outs):
            out_ref[:, at : at + size] = value[k * rows : (k + 1) * rows, :]


def products(lefts, near, far):
    lefts = [left if isinstance(left, list) else [left] for left in lefts]
    parts = [part for left in lefts for part in left]
    size = 2 * near.shape[0]
    rows = sum(part.shape[0] for part in lefts[0])
    width = near.shape[1]
    return pl.pallas_call(
        functools.partial(products_kernel, len(parts)),
        out_shape=(jax.ShapeDtypeStruct((rows, size), jnp.bfloat16),) * len(lefts),
        in_specs=[WHOLE] * (len(parts) + 2),
        out_specs=(WHOLE,) * len(lefts),
        scratch_shapes=[pltpu.VMEM((len(lefts) * rows, width), jnp.bfloat16)],
        compiler_params=pltpu.CompilerParams(vmem_limit_bytes=12 * 1024 * 1024),
        cost_estimate=pl.CostEstimate(flops=0, bytes_accessed=size, transcendentals=0),
    )(*parts, near, far)


def finish_kernel(line, place_ref, *refs):
    blocks = refs[: line * SIDES]
    factor_ref, wtile_ref, sigma_ref, tiles_ref = refs[line * SIDES :]
    rows = factor_ref.shape[0]
    width = sigma_ref.shape[1] // 2
    spot, core = place_ref[0], place_ref[1]
    total = wtile_ref[...].astype(jnp.float32)
    for d, ref in enumerate(blocks):
        at = lax.rem(spot + d, line * SIDES)
        chip = jnp.where(at < line, at * SIDES, (2 * line - 1 - at) * SIDES + 1)
        for turn in range(CORES):
            owner = core if turn == 0 else 1 - core
            for half in range(2):
                lane = (chip * CORES + owner) * rows + half * width
                lanes = pl.ds(pl.multiple_of(lane, TILE), rows)
                group = turn * 2 + half
                part = ref[:, group * rows : (group + 1) * rows]
                sigma_ref[:, lanes] = part.astype(jnp.float32)
                total -= contract_last(part, factor_ref[:, lanes])
    tiles_ref[...] = total


def finish(place, blocks, factor, wtile):
    rows = factor.shape[0]
    return pl.pallas_call(
        functools.partial(finish_kernel, len(blocks) // SIDES),
        out_shape=(
            jax.ShapeDtypeStruct(factor.shape, jnp.float32),
            jax.ShapeDtypeStruct((rows, TILE), jnp.float32),
        ),
        in_specs=[SCALAR] + [WHOLE] * (len(blocks) + 2),
        out_specs=(WHOLE, WHOLE),
        compiler_params=pltpu.CompilerParams(vmem_limit_bytes=10 * 1024 * 1024),
        cost_estimate=pl.CostEstimate(flops=0, bytes_accessed=rows, transcendentals=0),
    )(place, *blocks, factor, wtile)


def shards(ring, inverse_block, coupling_tiles, tile_pos, sep_diag, sep_cross):
    wrows = inverse_block[0]
    rows, width = wrows.shape
    tiles = coupling_tiles[0]
    per_shard = tiles.shape[0]
    diag = sep_diag[0]
    cross = sep_cross[0]
    index = lax.axis_index("rows")
    core = index % CORES
    chip = index // CORES
    far_side = chip % SIDES == 1
    spot = jnp.where(far_side, ring.count - 1 - chip // SIDES, chip // SIDES)

    half = ring.line // 2
    shifts = [0] + [sign * k for k in range(1, half) for sign in (1, -1)] + [half]
    along = (chip // SIDES + jnp.asarray(shifts * SIDES, jnp.int32)) % ring.line
    sides = jnp.asarray([side for side in range(SIDES) for _ in shifts], jnp.int32)
    chips = along * SIDES + (sides ^ (chip % SIDES))
    place = jnp.concatenate([spot[None], core[None], chips]).astype(jnp.int32)

    size = lax.axis_size("tm")
    steps = ring.count // 2
    plain = tiles.reshape(-1, TILE)
    wahead, wbehind = [wrows, ring.turn(wrows, 1)], [wrows, ring.turn(wrows, -1)]
    second = [ring.turn(wahead[1], 1), ring.turn(wbehind[1], -1)]
    following = lax.ppermute(diag, "tm", [(i + 1, i) for i in range(size - 1)])
    flipped = flip(tile_pos[0], cross)
    pieces = {0: plain, 1: ring.move(plain, -1), -1: ring.move(plain, 1)}
    sides = {0: ring.move(plain, 0, 1)}
    pieces[1], pieces[-1], sides[0], flipped, place = lax.optimization_barrier(
        (pieces[1], pieces[-1], sides[0], flipped, place)
    )
    cols = lax.all_to_all(flipped, "rows", 0, 0, tiled=True)
    for k in range(2, half):
        pieces[k], pieces[-k] = ring.move(pieces[k - 1], -1), ring.move(pieces[1 - k], 1)
    pieces[half] = ring.move(pieces[half - 1], -1)
    for k in shifts[1:-1]:
        sides[k] = ring.move(pieces[k], 0, 1)
    pieces[half], *back = lax.optimization_barrier(
        (pieces[half], *[sides[k] for k in shifts[1:-1]])
    )
    sides.update(zip(shifts[1:-1], back))
    sides[half] = ring.move(pieces[half], 0, 1)
    sides[half], wahead[1], wbehind[1], following = lax.optimization_barrier(
        (sides[half], wahead[1], wbehind[1], following)
    )
    pieces = [pieces[k] for k in shifts] + [sides[k] for k in shifts]
    wahead.append(second[0])
    wbehind.append(second[1])
    near = jnp.concatenate(pieces, axis=0)
    far = ring.to_core(near)

    first, marks = rows, cols
    if rows < TILE:
        first, marks = 0, cols[:, rows:, :]
        cols = cols[:, :rows, :].reshape(width // TILE, TILE // rows, rows, rows)
        cols = cols.transpose(0, 2, 1, 3).reshape(width // TILE, rows, TILE)
    updated = update(ring.line, first, place, near, far, marks, diag, cross, cols, following)
    updated, wahead[2], wbehind[2] = lax.optimization_barrier((updated, wahead[2], wbehind[2]))
    for step in range(3, steps):
        wahead.append(ring.turn(wahead[-1], 1))
        wbehind.append(ring.turn(wbehind[-1], -1))
    other = ring.to_core(updated)
    factor = factor_rows(ring.line, first, place, near, far, marks, wrows)

    early = min(3, steps)
    lefts = [wrows]
    for step in range(1, early):
        lefts += [wahead[step], wbehind[step]]
    done = products(lefts, updated, other)
    blocks = [done[0]] + [None] * (ring.count - 1)
    for step in range(1, early):
        blocks[step] = ring.turn(done[2 * step - 1], -step)
        blocks[-step] = ring.turn(done[2 * step], step)
        if step == 1:
            blocks[1], blocks[-1], wahead[-1], wbehind[-1] = lax.optimization_barrier(
                (blocks[1], blocks[-1], wahead[-1], wbehind[-1])
            )
    last = ring.opposite(wahead[-1], wbehind[-1])
    for step in range(early, steps):
        pair = products([wahead[step], wbehind[step]], updated, other)
        blocks[step] = ring.turn(pair[0], -step)
        blocks[-step] = ring.turn(pair[1], step)
    blocks[steps] = ring.turn(products([last], updated, other)[0], steps)

    if rows == TILE:
        wtile = lax.dynamic_slice_in_dim(wrows, index * rows, rows, 1)
        sigma, result = finish(place, blocks, factor, wtile)
        return (sigma[None], result[None])
    order = (jnp.asarray(ring.spots, jnp.int32) - spot) % ring.count
    parts = jnp.take(jnp.stack(blocks), order, axis=0)
    parts = parts.reshape(ring.count, rows, CORES, 2, rows)
    parts = jnp.where(core == 0, parts, parts[:, :, ::-1])
    rounded = parts.transpose(1, 3, 0, 2, 4).reshape(rows, 2 * width)
    sigma = rounded.astype(jnp.float32)
    if rows < TILE:
        whole = factor
        for bit in range((TILE // rows).bit_length() - 1):
            pairs = [(i, i ^ 1 << bit) for i in range(lax.axis_size("rows"))]
            partner = lax.ppermute(whole, "rows", pairs)
            whole = jnp.where(
                index >> bit & 1 == 0,
                jnp.concatenate([whole, partner], axis=0),
                jnp.concatenate([partner, whole], axis=0),
            )
        overlap = contract_last(rounded, whole)
        start = index * rows // TILE * TILE
        wtile = lax.dynamic_slice_in_dim(wrows, start, TILE, 1).astype(jnp.float32)
        result_tiles = wtile - overlap
    else:
        many = rows // TILE
        overlap = jnp.einsum(
            "mrk,mck->mrc",
            rounded.reshape(many, TILE, 2 * width),
            factor.reshape(many, TILE, 2 * width),
            preferred_element_type=jnp.float32,
        )
        square = lax.dynamic_slice_in_dim(wrows, index * rows, rows, 1).reshape(
            many, TILE, many, TILE
        )
        wtile = jnp.stack([square[i, :, i, :] for i in range(many)]).astype(jnp.float32)
        result_tiles = (wtile - overlap).reshape(rows, TILE)
    return (sigma[None], result_tiles[None])


def solution(mesh):
    placed = (
        P("tm", "rows", None),
        P("tm", "rows", None, None),
        P("tm", "rows", None),
        P("tm", "rows", None),
        P("tm", "rows", None),
    )
    return jax.shard_map(
        functools.partial(shards, Ring(mesh.shape["rows"])),
        mesh=mesh,
        in_specs=placed,
        out_specs=(P("tm", "rows", None), P("tm", "rows", None)),
        check_vma=False,
    )
```

```python
import functools

import jax
import jax.numpy as jnp
from jax import lax
from jax.experimental import pallas as pl
from jax.experimental.pallas import tpu as pltpu
from jax.sharding import PartitionSpec as P

TILE = 128
PAD = 16
SIDES = 2
CORES = 2

WHOLE = pl.BlockSpec(memory_space=pltpu.VMEM)
SCALAR = pl.BlockSpec(memory_space=pltpu.SMEM)
ANY = pl.BlockSpec(memory_space=pl.ANY)


def contract_last(left, right):
    return lax.dot_general(
        left, right, (((1,), (1,)), ((), ())), preferred_element_type=jnp.float32
    )


class Ring:
    def __init__(self, devices):
        self.line = devices // (SIDES * CORES)
        self.count = self.line * SIDES
        ups = [(z, 0) for z in range(self.line)]
        downs = [(z, 1) for z in reversed(range(self.line))]
        self.chips = [z * SIDES + y for z, y in ups + downs]
        self.spots = [self.chips.index(chip) for chip in range(self.count)]

    def turn(self, part, by):
        pairs = []
        for at, chip in enumerate(self.chips):
            target = self.chips[(at + by) % self.count]
            pairs += [(chip * CORES + c, target * CORES + c) for c in range(CORES)]
        return lax.ppermute(part, "rows", pairs)

    def move(self, part, by, cross=0):
        pairs = []
        for z in range(self.line):
            for y in range(SIDES):
                source = (z * SIDES + y) * CORES
                target = ((z + by) % self.line * SIDES + (y ^ cross)) * CORES
                pairs += [(source + c, target + c) for c in range(CORES)]
        return lax.ppermute(part, "rows", pairs)

    def to_core(self, part):
        devices = self.count * CORES
        return lax.ppermute(part, "rows", [(i, i ^ 1) for i in range(devices)])

    def opposite(self, ahead, behind):
        half = ahead.shape[0] // 2
        return [self.turn(ahead[:half], 1), self.turn(behind[half:], -1)]


def flip_kernel(pos_ref, cross_ref, out_ref):
    devices, _, rows = out_ref.shape
    lane = lax.broadcasted_iota(jnp.int32, (PAD, rows), 1)
    marks = jnp.zeros((PAD, rows), jnp.int32)
    for k in range(pos_ref.shape[0]):
        marks = jnp.where(lane == 2 * k, pos_ref[k, 0], marks)
        marks = jnp.where(lane == 2 * k + 1, pos_ref[k, 1], marks)
    marks = marks.astype(jnp.float32).astype(jnp.bfloat16)
    for i in range(devices):
        out_ref[i, :rows, :] = cross_ref[:, i * rows : (i + 1) * rows].T
        out_ref[i, rows:, :] = marks


def flip(positions, cross):
    rows, width = cross.shape
    return pl.pallas_call(
        flip_kernel,
        out_shape=jax.ShapeDtypeStruct((width // rows, rows + PAD, rows), jnp.bfloat16),
        in_specs=[SCALAR, WHOLE],
        out_specs=WHOLE,
        compiler_params=pltpu.CompilerParams(vmem_limit_bytes=6 * 1024 * 1024),
        cost_estimate=pl.CostEstimate(flops=0, bytes_accessed=rows, transcendentals=0),
    )(positions, cross)


def read_marks(marks_in, first, marks_ref, pos_ref, pos_sem):
    devices, _, lanes = marks_in.shape
    for i in range(devices):
        row = marks_in[i, first : first + PAD, :].astype(jnp.float32).astype(jnp.int32)
        marks_ref[i, :, :lanes] = row[:8]
    fetch = pltpu.make_async_copy(marks_ref, pos_ref, pos_sem)
    fetch.start()
    return fetch


def each_tile(line, place_ref, near_ref, far_ref, pos_ref, add):
    core = place_ref[1]
    count = line * SIDES
    per_shard = near_ref.shape[0] // (count * TILE)

    @pl.loop(0, count)
    def _(s):
        chip = place_ref[2 + s]
        for turn, ref in enumerate((near_ref, far_ref)):
            source = chip * CORES + (core if turn == 0 else 1 - core)
            for t in range(per_shard):
                start = pl.multiple_of((s * per_shard + t) * TILE, TILE)
                tile = ref[pl.ds(start, TILE), :]
                add(tile, pos_ref[source, 0, 2 * t], pos_ref[source, 0, 2 * t + 1])


def mark_scratch(devices):
    return [
        pltpu.VMEM((devices, 8, TILE), jnp.int32),
        pltpu.SMEM((devices, 8, TILE), jnp.int32),
        pltpu.SemaphoreType.DMA,
    ]


def update_kernel(
    line,
    first,
    place_ref,
    near_ref,
    far_ref,
    marks_in,
    diag_in,
    cross_in,
    cols_ref,
    next_in,
    out_ref,
    sep_ref,
    sum_ref,
    loaded_ref,
    sems,
    marks_ref,
    pos_ref,
    pos_sem,
):
    loads = []
    for k, source in enumerate((diag_in, cross_in, next_in)):
        loads.append(pltpu.make_async_copy(source, loaded_ref.at[k], sems.at[k]))
        loads[-1].start()
    fetch = read_marks(marks_in, first, marks_ref, pos_ref, pos_sem)
    sum_ref[...] = jnp.zeros_like(sum_ref)
    for load in loads:
        load.wait()
    _, rows, width = loaded_ref.shape
    count = width // TILE
    for j in range(count):
        lanes = slice(j * TILE, (j + 1) * TILE)
        sep_ref[j, :rows, :] = loaded_ref[0, :, lanes]
        sep_ref[j, rows:, :] = cols_ref[j, :rows, :]
        sep_ref[count + j, :rows, :] = loaded_ref[1, :, lanes]
        sep_ref[count + j, rows:, :] = loaded_ref[2, :, lanes]
    fetch.wait()

    def add(tile, i, j):
        sum_ref[i] += contract_last(sep_ref[j], tile)

    each_tile(line, place_ref, near_ref, far_ref, pos_ref, add)
    for i in range(count):
        out_ref[:, i * TILE : (i + 1) * TILE] = sum_ref[i].astype(jnp.bfloat16)


def update(line, first, place, near, far, marks, diag, cross, cols, following):
    rows, width = diag.shape
    count = width // TILE
    return pl.pallas_call(
        functools.partial(update_kernel, line, first),
        out_shape=jax.ShapeDtypeStruct((2 * rows, width), jnp.bfloat16),
        in_specs=[SCALAR] + [WHOLE] * 3 + [ANY, ANY, WHOLE, ANY],
        out_specs=WHOLE,
        scratch_shapes=[
            pltpu.VMEM((2 * count, 2 * rows, TILE), jnp.bfloat16),
            pltpu.VMEM((count, 2 * rows, TILE), jnp.float32),
            pltpu.VMEM((3, rows, width), jnp.bfloat16),
            pltpu.SemaphoreType.DMA((3,)),
        ]
        + mark_scratch(marks.shape[0]),
        compiler_params=pltpu.CompilerParams(vmem_limit_bytes=54 * 1024 * 1024),
        cost_estimate=pl.CostEstimate(flops=0, bytes_accessed=rows, transcendentals=0),
    )(place, near, far, marks, diag, cross, cols, following)


def factor_kernel(
    line,
    first,
    place_ref,
    near_ref,
    far_ref,
    marks_in,
    wrows_ref,
    out_ref,
    wtile_ref,
    sum_ref,
    marks_ref,
    pos_ref,
    pos_sem,
):
    fetch = read_marks(marks_in, first, marks_ref, pos_ref, pos_sem)
    count = wrows_ref.shape[1] // TILE
    for j in range(count):
        wtile_ref[j] = wrows_ref[:, j * TILE : (j + 1) * TILE]
    sum_ref[...] = jnp.zeros_like(sum_ref)
    fetch.wait()

    def add(tile, i, j):
        sum_ref[j] += jnp.dot(wtile_ref[i], tile, preferred_element_type=jnp.float32)

    each_tile(line, place_ref, near_ref, far_ref, pos_ref, add)
    for j in range(2 * count):
        out_ref[:, j * TILE : (j + 1) * TILE] = sum_ref[j].astype(jnp.bfloat16)


def factor_rows(line, first, place, near, far, marks, wrows):
    rows, width = wrows.shape
    count = width // TILE
    return pl.pallas_call(
        functools.partial(factor_kernel, line, first),
        out_shape=jax.ShapeDtypeStruct((rows, 2 * width), jnp.bfloat16),
        in_specs=[SCALAR] + [WHOLE] * 4,
        out_specs=WHOLE,
        scratch_shapes=[
            pltpu.VMEM((count, rows, TILE), jnp.bfloat16),
            pltpu.VMEM((2 * count, rows, TILE), jnp.float32),
        ]
        + mark_scratch(marks.shape[0]),
        compiler_params=pltpu.CompilerParams(vmem_limit_bytes=8 * 1024 * 1024),
        cost_estimate=pl.CostEstimate(flops=0, bytes_accessed=rows, transcendentals=0),
    )(place, near, far, marks, wrows)


def products_kernel(many, *refs):
    lefts, (near_ref, far_ref), outs = refs[:many], refs[many : many + 2], refs[many + 2 : -1]
    all_ref = refs[-1]
    size = near_ref.shape[0]
    at = 0
    for left_ref in lefts:
        all_ref[at : at + left_ref.shape[0], :] = left_ref[...]
        at += left_ref.shape[0]
    rows = outs[0].shape[0]
    for at, ref in ((0, near_ref), (size, far_ref)):
        value = (-contract_last(all_ref[...], ref[...])).astype(jnp.bfloat16)
        for k, out_ref in enumerate(outs):
            out_ref[:, at : at + size] = value[k * rows : (k + 1) * rows, :]


def products(lefts, near, far):
    lefts = [left if isinstance(left, list) else [left] for left in lefts]
    parts = [part for left in lefts for part in left]
    size = 2 * near.shape[0]
    rows = sum(part.shape[0] for part in lefts[0])
    width = near.shape[1]
    return pl.pallas_call(
        functools.partial(products_kernel, len(parts)),
        out_shape=(jax.ShapeDtypeStruct((rows, size), jnp.bfloat16),) * len(lefts),
        in_specs=[WHOLE] * (len(parts) + 2),
        out_specs=(WHOLE,) * len(lefts),
        scratch_shapes=[pltpu.VMEM((len(lefts) * rows, width), jnp.bfloat16)],
        compiler_params=pltpu.CompilerParams(vmem_limit_bytes=12 * 1024 * 1024),
        cost_estimate=pl.CostEstimate(flops=0, bytes_accessed=size, transcendentals=0),
    )(*parts, near, far)


def finish_kernel(line, place_ref, *refs):
    blocks = refs[: line * SIDES]
    factor_ref, wtile_ref, sigma_ref, tiles_ref = refs[line * SIDES :]
    rows = factor_ref.shape[0]
    width = sigma_ref.shape[1] // 2
    spot, core = place_ref[0], place_ref[1]
    total = wtile_ref[...].astype(jnp.float32)
    for d, ref in enumerate(blocks):
        at = lax.rem(spot + d, line * SIDES)
        chip = jnp.where(at < line, at * SIDES, (2 * line - 1 - at) * SIDES + 1)
        for turn in range(CORES):
            owner = core if turn == 0 else 1 - core
            for half in range(2):
                lane = (chip * CORES + owner) * rows + half * width
                lanes = pl.ds(pl.multiple_of(lane, TILE), rows)
                group = turn * 2 + half
                part = ref[:, group * rows : (group + 1) * rows]
                sigma_ref[:, lanes] = part.astype(jnp.float32)
                total -= contract_last(part, factor_ref[:, lanes])
    tiles_ref[...] = total


def finish(place, blocks, factor, wtile):
    rows = factor.shape[0]
    return pl.pallas_call(
        functools.partial(finish_kernel, len(blocks) // SIDES),
        out_shape=(
            jax.ShapeDtypeStruct(factor.shape, jnp.float32),
            jax.ShapeDtypeStruct((rows, TILE), jnp.float32),
        ),
        in_specs=[SCALAR] + [WHOLE] * (len(blocks) + 2),
        out_specs=(WHOLE, WHOLE),
        compiler_params=pltpu.CompilerParams(vmem_limit_bytes=10 * 1024 * 1024),
        cost_estimate=pl.CostEstimate(flops=0, bytes_accessed=rows, transcendentals=0),
    )(place, *blocks, factor, wtile)


def shards(ring, inverse_block, coupling_tiles, tile_pos, sep_diag, sep_cross):
    wrows = inverse_block[0]
    rows, width = wrows.shape
    tiles = coupling_tiles[0]
    per_shard = tiles.shape[0]
    diag = sep_diag[0]
    cross = sep_cross[0]
    index = lax.axis_index("rows")
    core = index % CORES
    chip = index // CORES
    far_side = chip % SIDES == 1
    spot = jnp.where(far_side, ring.count - 1 - chip // SIDES, chip // SIDES)

    half = ring.line // 2
    shifts = [0] + [sign * k for k in range(1, half) for sign in (1, -1)] + [half]
    along = (chip // SIDES + jnp.asarray(shifts * SIDES, jnp.int32)) % ring.line
    sides = jnp.asarray([side for side in range(SIDES) for _ in shifts], jnp.int32)
    chips = along * SIDES + (sides ^ (chip % SIDES))
    place = jnp.concatenate([spot[None], core[None], chips]).astype(jnp.int32)

    size = lax.axis_size("tm")
    steps = ring.count // 2
    plain = tiles.reshape(-1, TILE)
    wahead, wbehind = [wrows, ring.turn(wrows, 1)], [wrows, ring.turn(wrows, -1)]
    second = [ring.turn(wahead[1], 1), ring.turn(wbehind[1], -1)]
    following = lax.ppermute(diag, "tm", [((i + 1) % size, i) for i in range(size)])
    flipped = flip(tile_pos[0], cross)
    pieces = {0: plain, 1: ring.move(plain, -1), -1: ring.move(plain, 1)}
    sides = {0: ring.move(plain, 0, 1)}
    pieces[1], pieces[-1], sides[0], flipped, place = lax.optimization_barrier(
        (pieces[1], pieces[-1], sides[0], flipped, place)
    )
    cols = lax.all_to_all(flipped, "rows", 0, 0, tiled=True)
    for k in range(2, half):
        pieces[k], pieces[-k] = ring.move(pieces[k - 1], -1), ring.move(pieces[1 - k], 1)
    pieces[half] = ring.move(pieces[half - 1], -1)
    for k in shifts[1:-1]:
        sides[k] = ring.move(pieces[k], 0, 1)
    pieces[half], *back = lax.optimization_barrier(
        (pieces[half], *[sides[k] for k in shifts[1:-1]])
    )
    sides.update(zip(shifts[1:-1], back))
    sides[half] = ring.move(pieces[half], 0, 1)
    sides[half], wahead[1], wbehind[1], following = lax.optimization_barrier(
        (sides[half], wahead[1], wbehind[1], following)
    )
    pieces = [pieces[k] for k in shifts] + [sides[k] for k in shifts]
    wahead.append(second[0])
    wbehind.append(second[1])
    near = jnp.concatenate(pieces, axis=0)
    far = ring.to_core(near)

    first, marks = rows, cols
    if rows < TILE:
        first, marks = 0, cols[:, rows:, :]
        cols = cols[:, :rows, :].reshape(width // TILE, TILE // rows, rows, rows)
        cols = cols.transpose(0, 2, 1, 3).reshape(width // TILE, rows, TILE)
    following = jnp.where(lax.axis_index("tm") == size - 1, jnp.zeros_like(diag), following)
    updated = update(ring.line, first, place, near, far, marks, diag, cross, cols, following)
    updated, wahead[2], wbehind[2] = lax.optimization_barrier((updated, wahead[2], wbehind[2]))
    for step in range(3, steps):
        wahead.append(ring.turn(wahead[-1], 1))
        wbehind.append(ring.turn(wbehind[-1], -1))
    other = ring.to_core(updated)
    factor = factor_rows(ring.line, first, place, near, far, marks, wrows)

    early = min(3, steps)
    lefts = [wrows]
    for step in range(1, early):
        lefts += [wahead[step], wbehind[step]]
    done = products(lefts, updated, other)
    blocks = [done[0]] + [None] * (ring.count - 1)
    for step in range(1, early):
        blocks[step] = ring.turn(done[2 * step - 1], -step)
        blocks[-step] = ring.turn(done[2 * step], step)
        if step == 1:
            blocks[1], blocks[-1], wahead[-1], wbehind[-1] = lax.optimization_barrier(
                (blocks[1], blocks[-1], wahead[-1], wbehind[-1])
            )
    last = ring.opposite(wahead[-1], wbehind[-1])
    for step in range(early, steps):
        pair = products([wahead[step], wbehind[step]], updated, other)
        blocks[step] = ring.turn(pair[0], -step)
        blocks[-step] = ring.turn(pair[1], step)
    blocks[steps] = ring.turn(products([last], updated, other)[0], steps)

    if rows == TILE:
        wtile = lax.dynamic_slice_in_dim(wrows, index * rows, rows, 1)
        sigma, result = finish(place, blocks, factor, wtile)
        return (sigma[None], result[None])
    order = (jnp.asarray(ring.spots, jnp.int32) - spot) % ring.count
    parts = jnp.take(jnp.stack(blocks), order, axis=0)
    parts = parts.reshape(ring.count, rows, CORES, 2, rows)
    parts = jnp.where(core == 0, parts, parts[:, :, ::-1])
    rounded = parts.transpose(1, 3, 0, 2, 4).reshape(rows, 2 * width)
    sigma = rounded.astype(jnp.float32)
    if rows < TILE:
        whole = factor
        for bit in range((TILE // rows).bit_length() - 1):
            pairs = [(i, i ^ 1 << bit) for i in range(lax.axis_size("rows"))]
            partner = lax.ppermute(whole, "rows", pairs)
            whole = jnp.where(
                index >> bit & 1 == 0,
                jnp.concatenate([whole, partner], axis=0),
                jnp.concatenate([partner, whole], axis=0),
            )
        overlap = contract_last(rounded, whole)
        start = index * rows // TILE * TILE
        wtile = lax.dynamic_slice_in_dim(wrows, start, TILE, 1).astype(jnp.float32)
        result_tiles = wtile - overlap
    else:
        many = rows // TILE
        overlap = jnp.einsum(
            "mrk,mck->mrc",
            rounded.reshape(many, TILE, 2 * width),
            factor.reshape(many, TILE, 2 * width),
            preferred_element_type=jnp.float32,
        )
        square = lax.dynamic_slice_in_dim(wrows, index * rows, rows, 1).reshape(
            many, TILE, many, TILE
        )
        wtile = jnp.stack([square[i, :, i, :] for i in range(many)]).astype(jnp.float32)
        result_tiles = (wtile - overlap).reshape(rows, TILE)
    return (sigma[None], result_tiles[None])


def solution(mesh):
    placed = (
        P("tm", "rows", None),
        P("tm", "rows", None, None),
        P("tm", "rows", None),
        P("tm", "rows", None),
        P("tm", "rows", None),
    )
    return jax.shard_map(
        functools.partial(shards, Ring(mesh.shape["rows"])),
        mesh=mesh,
        in_specs=placed,
        out_specs=(P("tm", "rows", None), P("tm", "rows", None)),
        check_vma=False,
    )
```
